32 devices in a mesh: dp: 8 (over z, y), tensor: 4 (over x, core).
Axes of the slice: x: 2, y: 2, z: 4, core: 2. Of those that a mesh axis runs over, the one named last changes fastest.
Arguments:
- tokens: bfloat16 [8, 1024, 1280], P('dp', 'tensor'), may hold values from -6 to 6
- prefix: int32 [8], P('dp'), may hold values from 102 to 512, as said below
- cotangent: bfloat16 [8, 1024, 1280], P('dp', 'tensor'), may hold values from -6 to 6
- query_weight: float32 [1280, 1280], P('dp', 'tensor'), may hold values from -0.15625 to 0.15625
- query_first: float32 [1280, 1280], P('dp', 'tensor')
- query_second: float32 [1280, 1280], P('dp', 'tensor'), as said below
- keyval_weight: float32 [1280, 640], P('dp'), may hold values from -0.15625 to 0.15625
- keyval_first: float32 [1280, 640], P('dp')
- keyval_second: float32 [1280, 640], P('dp'), as said below
- outproj_weight: float32 [1280, 1280], P('tensor', 'dp'), may hold values from -0.625 to 0.625
- outproj_first: float32 [1280, 1280], P('tensor', 'dp')
- outproj_second: float32 [1280, 1280], P('tensor', 'dp'), as said below
- gate_up_weight: float32 [2, 1280, 3584], P(None, 'dp', 'tensor')
- gate_up_first: float32 [2, 1280, 3584], P(None, 'dp', 'tensor')
- gate_up_second: float32 [2, 1280, 3584], P(None, 'dp', 'tensor'), as said below
- down_weight: float32 [3584, 1280], P('tensor', 'dp'), may hold values from -0.09375 to 0.09375
- down_first: float32 [3584, 1280], P('tensor', 'dp')
- down_second: float32 [3584, 1280], P('tensor', 'dp'), as said below
- norm_gains: float32 [2, 1280], P(None, 'dp'), as said below
- gains_first: float32 [2, 1280], P(None, 'dp')
- gains_second: float32 [2, 1280], P(None, 'dp'), as said below
Outputs:
- output: bfloat16 [8, 1024, 1280], P('dp', 'tensor')
- input_grad: float32 [8, 1024, 1280], P('dp', 'tensor')
- query_first_new: float32 [1280, 1280], P('dp', 'tensor')
- query_second_new: float32 [1280, 1280], P('dp', 'tensor')
- query_new: float32 [1280, 1280], P('dp', 'tensor')
- keyval_first_new: float32 [1280, 640], P('dp')
- keyval_second_new: float32 [1280, 640], P('dp')
- keyval_new: float32 [1280, 640], P('dp')
- outproj_first_new: float32 [1280, 1280], P('tensor', 'dp')
- outproj_second_new: float32 [1280, 1280], P('tensor', 'dp')
- outproj_new: float32 [1280, 1280], P('tensor', 'dp')
- gate_up_first_new: float32 [2, 1280, 3584], P(None, 'dp', 'tensor')
- gate_up_second_new: float32 [2, 1280, 3584], P(None, 'dp', 'tensor')
- gate_up_new: float32 [2, 1280, 3584], P(None, 'dp', 'tensor')
- down_first_new: float32 [3584, 1280], P('tensor', 'dp')
- down_second_new: float32 [3584, 1280], P('tensor', 'dp')
- down_new: float32 [3584, 1280], P('tensor', 'dp')
- gains_first_new: float32 [2, 1280], P(None, 'dp')
- gains_second_new: float32 [2, 1280], P(None, 'dp')
- gains_new: float32 [2, 1280], P(None, 'dp')
- grad_norm: float32 [], replicated
The draws below stay inside these ranges and needn't reach their ends.
Inputs may be any that keep to these rules, and one draw needn't show every extreme that they name: Every query of a sequence sees that sequence's positions below its prefix length; some sequence has the smallest and some the largest value. `query_second`: positive. `keyval_second`: positive. `outproj_second`: positive. `gate_up_second`: positive. `down_second`: positive. `gains_second`: positive. `norm_gains`: positive.
All inputs are finite; a program needn't handle non-finite values.
Results may differ from the reference program's by a relative error of at most 0.017.
The reference program's roundings to bfloat16 on the way count: a program that leaves them out, or rounds other values in their place, can miss the bound.
Values may be sent and summed in bfloat16 or wider, within the bound.
No kernel may reach another device: no remote copies, remote signals or barrier semaphores. Data moves between devices by JAX's collectives and lax.ppermute only.
A program may use at most 192 MiB of HBM per device.

```python
import math
import jax
import jax.numpy as jnp
from jax import lax

D = 1280
HEADS = 20
KV = 5
HD = 64
FF = 3584
LEN = 1024
STEP = 5
SEQS = 8
TOKENS = 8192
N_TENSOR = 4


def grad_size(factor):
    return 0.022 * factor * math.sqrt(TOKENS)


def first_moment(key, array_shape, factor):
    return jax.random.normal(key, array_shape, jnp.float32) * grad_size(factor)


def second_moment(key, array_shape, factor):
    spread = jnp.exp(jax.random.uniform(key, array_shape, jnp.float32, math.log(0.5), math.log(2.0)))
    return spread * (2.0 * (0.4 / 0.6) * grad_size(factor) ** 2)


def draw_prefix(key, part):
    key = jax.random.fold_in(key, 11)
    lowest = LEN // 10
    highest = LEN // 2
    values = jax.random.randint(key, (SEQS,), lowest, highest + 1, dtype=jnp.int32)
    shuffled = jax.random.permutation(jax.random.fold_in(key, 1), SEQS)
    return values.at[shuffled[0]].set(lowest).at[shuffled[1]].set(highest)


def draw_norm_gains(key, part):
    key = jax.random.fold_in(key, 5)
    ramp = jnp.arange(D, dtype=jnp.float32) / D
    base_line = 0.6 + 1.2 * ramp
    jitter = jax.random.uniform(key, (2, D), jnp.float32, 0.8, 1.25)
    return base_line[None, :] * jitter


def draw_gate_up_weight(key, part):
    key = jax.random.fold_in(key, 7)
    column = jnp.arange(FF, dtype=jnp.float32) / FF
    noise = jax.random.normal(key, (2, D, FF), jnp.float32)
    ramp = 0.7 * 2.0 ** column
    return noise * ramp[None, None, :] / math.sqrt(D)


def draw_query_first(key, part):
    key = jax.random.fold_in(key, 21)
    return first_moment(key, (D, HEADS * HD), 0.3)


def draw_query_second(key, part):
    key = jax.random.fold_in(key, 22)
    return second_moment(key, (D, HEADS * HD), 0.3)


def draw_keyval_first(key, part):
    key = jax.random.fold_in(key, 23)
    return first_moment(key, (D, 2 * KV * HD), 0.5)


def draw_keyval_second(key, part):
    key = jax.random.fold_in(key, 24)
    return second_moment(key, (D, 2 * KV * HD), 0.5)


def draw_outproj_first(key, part):
    key = jax.random.fold_in(key, 25)
    return first_moment(key, (HEADS * HD, D), 0.3)


def draw_outproj_second(key, part):
    key = jax.random.fold_in(key, 26)
    return second_moment(key, (HEADS * HD, D), 0.3)


def draw_gate_up_first(key, part):
    key = jax.random.fold_in(key, 27)
    return first_moment(key, (2, D, FF), 0.4)


def draw_gate_up_second(key, part):
    key = jax.random.fold_in(key, 28)
    return second_moment(key, (2, D, FF), 0.4)


def draw_down_first(key, part):
    key = jax.random.fold_in(key, 29)
    return first_moment(key, (FF, D), 0.6)


def draw_down_second(key, part):
    key = jax.random.fold_in(key, 30)
    return second_moment(key, (FF, D), 0.6)


def draw_gains_first(key, part):
    key = jax.random.fold_in(key, 31)
    return first_moment(key, (2, D), 1.0)


def draw_gains_second(key, part):
    key = jax.random.fold_in(key, 32)
    return second_moment(key, (2, D), 1.0)


def steps_of(stream_key, extent, shards, least, top_value):
    level = 1.0
    for dim, blocks in shards:
        steps = jax.random.uniform(jax.random.fold_in(jax.random.fold_in(stream_key, 6), dim), (blocks,), jnp.float32, least / len(shards), top_value / len(shards))
        level = level * jnp.repeat(jnp.exp(steps), extent[dim] // blocks).reshape((-1,) + (1,) * (len(extent) - 1 - dim))
    return level


def gaussian(stream_key, shape, scale, bound, split=(), held_as=jnp.bfloat16):
    values = scale * jax.random.normal(stream_key, shape, jnp.float32)
    if split:
        values = values * steps_of(stream_key, shape, split, -0.22, 0.18)
    return jnp.clip(values, -bound, bound).astype(held_as)


def setup_inputs(seed: int = 0) -> dict:
    keys = jax.random.split(jax.random.key(seed), 22)
    tokens = gaussian(keys[0], (SEQS, LEN, D), 1.0, 6.0, ((0, 8), (1, 4)))
    prefix = draw_prefix(jax.random.fold_in(keys[21], 71), 0)
    cotangent = gaussian(keys[2], (SEQS, LEN, D), 1.0, 6.0, ((0, 8), (1, 4)))
    query_weight = gaussian(keys[3], (D, HEADS * HD), D ** -0.5, 0.15625, ((0, 8), (1, 4)), jnp.float32)
    query_first = draw_query_first(jax.random.fold_in(keys[21], 71), 0)
    query_second = draw_query_second(jax.random.fold_in(keys[21], 71), 0)
    keyval_weight = gaussian(keys[6], (D, 2 * KV * HD), D ** -0.5, 0.15625, ((0, 8),), jnp.float32)
    keyval_first = draw_keyval_first(jax.random.fold_in(keys[21], 71), 0)
    keyval_second = draw_keyval_second(jax.random.fold_in(keys[21], 71), 0)
    outproj_weight = gaussian(keys[9], (HEADS * HD, D), (HEADS * HD // 16) ** -0.5, 0.625, ((0, 4), (1, 8)), jnp.float32)
    outproj_first = draw_outproj_first(jax.random.fold_in(keys[21], 71), 0)
    outproj_second = draw_outproj_second(jax.random.fold_in(keys[21], 71), 0)
    gate_up_weight = draw_gate_up_weight(jax.random.fold_in(keys[21], 71), 0)
    gate_up_first = draw_gate_up_first(jax.random.fold_in(keys[21], 71), 0)
    gate_up_second = draw_gate_up_second(jax.random.fold_in(keys[21], 71), 0)
    down_weight = gaussian(keys[15], (FF, D), FF ** -0.5, 0.09375, ((0, 4), (1, 8)), jnp.float32)
    down_first = draw_down_first(jax.random.fold_in(keys[21], 71), 0)
    down_second = draw_down_second(jax.random.fold_in(keys[21], 71), 0)
    norm_gains = draw_norm_gains(jax.random.fold_in(keys[21], 71), 0)
    gains_first = draw_gains_first(jax.random.fold_in(keys[21], 71), 0)
    gains_second = draw_gains_second(jax.random.fold_in(keys[21], 71), 0)
    return {"tokens": tokens, "prefix": prefix, "cotangent": cotangent, "query_weight": query_weight, "query_first": query_first, "query_second": query_second, "keyval_weight": keyval_weight, "keyval_first": keyval_first, "keyval_second": keyval_second, "outproj_weight": outproj_weight, "outproj_first": outproj_first, "outproj_second": outproj_second, "gate_up_weight": gate_up_weight, "gate_up_first": gate_up_first, "gate_up_second": gate_up_second, "down_weight": down_weight, "down_first": down_first, "down_second": down_second, "norm_gains": norm_gains, "gains_first": gains_first, "gains_second": gains_second}


EPSILON = 1e-05
BETA_ONE = 0.5
BETA_TWO = 0.6
ADAM_EPSILON = 1e-08
DECAY_RATE = 0.1
MASKED = -1e+30

@jax.custom_vjp
def low(v):
    return lax.optimization_barrier(v.astype(jnp.bfloat16)).astype(jnp.float32)

@jax.custom_vjp
def low_back(v):
    return v

def low_keep(v):
    return (low(v), None)

def low_pass(kept, grad):
    return (grad,)

def back_keep(v):
    return (v, None)

def back_low(kept, grad):
    return (low(grad),)
low.defvjp(low_keep, low_pass)
low_back.defvjp(back_keep, back_low)

def precise(left, right):
    return jnp.dot(left, right, precision=lax.Precision.HIGHEST, preferred_element_type=jnp.float32)

def rope_tables(length):
    position = jnp.arange(length, dtype=jnp.float32)
    frequency = 10000.0 ** (-(2.0 / HD) * jnp.arange(HD // 2, dtype=jnp.float32))
    angles = position[:, None] * frequency[None, :]
    return (jnp.cos(angles), jnp.sin(angles))

def rotate(values, cosine, sine_part):
    half_width = values.shape[-1] // 2
    first_half = values[..., :half_width]
    second_half = values[..., half_width:]
    return jnp.concatenate([first_half * cosine - second_half * sine_part, second_half * cosine + first_half * sine_part], axis=-1)

def root_norm(values, gain):
    scaled = values * lax.rsqrt(lax.optimization_barrier(jnp.mean(values * values, axis=-1, keepdims=True)) + EPSILON)
    return scaled * gain

def attend(query_rot, key_rot, value_low, prefix_len, length):
    rows_per = min(512, length)
    block_count = length // rows_per
    query_blocks = query_rot.reshape(block_count, rows_per, HEADS, HD)
    starts = jnp.arange(block_count, dtype=jnp.int32) * rows_per
    columns = jnp.arange(length, dtype=jnp.int32)

    def one_block(block_pair):
        query_block, block_start = block_pair
        rows_here = block_start + jnp.arange(rows_per, dtype=jnp.int32)
        raw = low_back(jnp.einsum('bhd,lhd->hbl', query_block, key_rot, precision=lax.Precision.HIGHEST))
        visible = (columns[None, :] <= rows_here[:, None]) | (columns[None, :] < prefix_len)
        scores = jnp.where(visible[None], raw * HD ** (-0.5), MASKED)
        highest = lax.optimization_barrier(jnp.max(scores, axis=-1, keepdims=True))
        totals = highest + jnp.log(lax.optimization_barrier(jnp.sum(jnp.exp(scores - highest), axis=-1, keepdims=True)))
        attn_probs = jnp.exp(scores - totals)
        return jnp.einsum('hbl,lhd->bhd', low(attn_probs), value_low, precision=lax.Precision.HIGHEST)
    attended = lax.map(jax.checkpoint(one_block), (query_blocks, starts))
    return attended.reshape(length, HEADS * HD)

def layer(hidden_in, weights, prefix_len):
    query_w, keyval_w, outproj_w, gate_up_w, down_w, gain_pair = weights
    length = hidden_in.shape[0]
    cosine, sine_part = rope_tables(length)
    cosine = cosine[:, None, :]
    sine_part = sine_part[:, None, :]
    gains_low = low(gain_pair)
    normed_one = low(root_norm(hidden_in, gains_low[0]))
    queries = low_back(precise(normed_one, low(query_w))).reshape(length, HEADS, HD)
    query_rot = low(rotate(queries, cosine, sine_part))
    keyval_low = low(keyval_w)
    group_heads = HEADS // N_TENSOR
    share_count = HEADS // KV
    key_parts = []
    value_parts = []
    for group in range(N_TENSOR):
        keyvals = low_back(precise(normed_one, keyval_low))
        keys_rot = low(rotate(keyvals[:, :KV * HD].reshape(length, KV, HD), cosine, sine_part))
        values_low = low(keyvals[:, KV * HD:].reshape(length, KV, HD))
        owners = jnp.asarray([(group * group_heads + head) // share_count for head in range(group_heads)], dtype=jnp.int32)
        key_parts.append(keys_rot[:, owners])
        value_parts.append(values_low[:, owners])
    key_rot = jnp.concatenate(key_parts, axis=1)
    value_low = jnp.concatenate(value_parts, axis=1)
    attended = attend(query_rot, key_rot, value_low, prefix_len, length)
    attn_low = low(low_back(attended))
    mixed_one = hidden_in + low_back(precise(attn_low, low(outproj_w)))
    normed_two = low(root_norm(mixed_one, gains_low[1]))
    gate_up_low = low(gate_up_w)
    gate = low_back(precise(normed_two, gate_up_low[0]))
    up_part = low_back(precise(normed_two, gate_up_low[1]))
    hidden_low = low(jax.nn.silu(gate) * up_part)
    return mixed_one + precise(hidden_low, low(down_w))

def adam_step(weight, first, second, gradient, rate, clip):
    clipped = gradient * clip
    first_new = BETA_ONE * first + (1.0 - BETA_ONE) * clipped
    second_new = BETA_TWO * second + (1.0 - BETA_TWO) * clipped * clipped
    corrected_one = first_new / (1.0 - BETA_ONE ** STEP)
    corrected_two = second_new / (1.0 - BETA_TWO ** STEP)
    weight_new = weight - rate * (corrected_one / (jnp.sqrt(corrected_two) + ADAM_EPSILON) + DECAY_RATE * weight)
    return (first_new, second_new, weight_new)

def reference(tokens, prefix, cotangent, query_weight, query_first, query_second, keyval_weight, keyval_first, keyval_second, outproj_weight, outproj_first, outproj_second, gate_up_weight, gate_up_first, gate_up_second, down_weight, down_first, down_second, norm_gains, gains_first, gains_second):
    weights = (query_weight, keyval_weight, outproj_weight, gate_up_weight, down_weight, norm_gains)
    inputs_all = tokens.astype(jnp.float32)
    cot_all = cotangent.astype(jnp.float32)

    def per_sequence(running, element):
        seq_in, seq_cot, seq_prefix = element

        def forward_fn(seq_values, *params):
            return layer(seq_values, params, seq_prefix)
        result, pullback = jax.vjp(forward_fn, seq_in, *weights)
        fresh = pullback(seq_cot)
        running = tuple((summed + addend for summed, addend in zip(running, fresh[1:])))
        return (running, (result.astype(jnp.bfloat16), fresh[0]))
    initial = tuple((jnp.zeros_like(weight) for weight in weights))
    totals, (output, input_grad) = lax.scan(per_sequence, initial, (inputs_all, cot_all, prefix))
    square_sum = sum((jnp.sum(entry * entry) for entry in totals))
    grad_norm = jnp.sqrt(square_sum)
    params_all = D * HEADS * HD + 2 * D * KV * HD + HEADS * HD * D + 2 * D * FF + FF * D + 2 * D
    limit = 0.01 * math.sqrt(TOKENS * params_all)
    clip = limit / jnp.maximum(grad_norm, limit)
    rates = (0.5 / math.sqrt(D), 0.5 / math.sqrt(D), 2.0 / math.sqrt(HEADS * HD), 0.5 / math.sqrt(D), 0.5 / math.sqrt(FF), 0.25)
    firsts = (query_first, keyval_first, outproj_first, gate_up_first, down_first, gains_first)
    seconds = (query_second, keyval_second, outproj_second, gate_up_second, down_second, gains_second)
    updates = [adam_step(weights[index], firsts[index], seconds[index], totals[index], rates[index], clip) for index in range(6)]
    return (output, input_grad, updates[0][0], updates[0][1], updates[0][2], updates[1][0], updates[1][1], updates[1][2], updates[2][0], updates[2][1], updates[2][2], updates[3][0], updates[3][1], updates[3][2], updates[4][0], updates[4][1], updates[4][2], updates[5][0], updates[5][1], updates[5][2], grad_norm)
```

```python
import functools
import math

import jax
import jax.numpy as jnp
import numpy as np
from jax import lax
from jax.experimental import pallas as pl
from jax.experimental.pallas import tpu as pltpu
from jax.sharding import PartitionSpec as P

D = 1280
HEADS = 20
KV = 5
HD = 64
FF = 3584
STEP = 5


EPSILON = 1e-05
BETA_ONE = 0.5
BETA_TWO = 0.6
ADAM_EPSILON = 1e-08
DECAY_RATE = 0.1
MASKED = -1e30

TENSOR = 4
GROUP = HEADS // TENSOR
SHARE = HEADS // KV
PAIR = 2
BLOCK = 256
PREFIX_MAX = 512
KV_COLS = 2 * PAIR * HD
Q_COLS = GROUP * HD
GAIN_COLS = 64
BF = jnp.bfloat16
F32 = jnp.float32


def rope_tables(length):
    position = np.arange(length, dtype=np.float32)
    frequency = (10000.0 ** (-(2.0 / HD) * np.arange(HD // 2))).astype(np.float32)
    angles = (frequency[:, None] * position[None, :]).astype(np.float32).astype(np.float64)
    return np.cos(angles).astype(np.float32), np.sin(angles).astype(np.float32)


def dot(left, right, left_dim, right_dim):
    return lax.dot_general(
        left, right, (((left_dim,), (right_dim,)), ((), ())), preferred_element_type=F32
    )


def norm_back(grad_normed, values_hat, inv_root, gain):
    scaled = grad_normed * gain
    return inv_root * (scaled - values_hat * jnp.mean(values_hat * scaled, axis=-1, keepdims=True))


def inverse_root(values):
    return lax.rsqrt(jnp.mean(values * values, axis=-1, keepdims=True) + EPSILON)


def adam_step(weight, first, second, gradient, rate, clip):
    clipped = gradient * clip
    first_new = BETA_ONE * first + (1.0 - BETA_ONE) * clipped
    second_new = BETA_TWO * second + (1.0 - BETA_TWO) * clipped * clipped
    corrected_one = first_new / (1.0 - BETA_ONE**STEP)
    corrected_two = second_new / (1.0 - BETA_TWO**STEP)
    weight_new = weight - rate * (
        corrected_one / (jnp.sqrt(corrected_two) + ADAM_EPSILON) + DECAY_RATE * weight
    )
    return (first_new, second_new, weight_new)


def swap(values, distance):
    return lax.ppermute(values, "tensor", [(i, i ^ distance) for i in range(TENSOR)])


def gather_blocks(rows):
    far = swap(rows, 2)
    near = swap(rows, 1)
    return [rows, near, far, swap(far, 1)]


def ring_order(count):
    return list(range(0, count, 2)) + list(range(count - 1, 0, -2))


OFFSETS = (0, -1, 1, -2, 2, -3, 3, 4)


def place_table(count):
    order = ring_order(count)
    table = np.zeros((count * TENSOR, 16), np.int32)
    for position, owner in enumerate(order):
        for group in range(TENSOR):
            row = table[owner * TENSOR + group]
            row[0] = group
            row[1 : 1 + len(OFFSETS)] = [order[(position + o) % count] for o in OFFSETS]
    return table


def ring_pass(values, step):
    order = ring_order(lax.axis_size("dp"))
    count = len(order)
    return lax.ppermute(
        values, "dp", [(order[q], order[(q + step) % count]) for q in range(count)]
    )


TRAIL = [None]
LIGHT = pl.CostEstimate(flops=1024, bytes_accessed=1024, transcendentals=0)


def in_order(name, deps, operands, build):
    deps = list(deps)
    last = TRAIL[0]
    if last is not None and all(last is not operand for operand in (*operands, *deps)):
        deps.append(last)
    result = build(deps)
    arrays = [array for array in result if array.size > 1]
    TRAIL[0] = arrays[0]
    return result


def call(
    name, body, outs, ins=(), scalars=(), deps=(), scratch=(), mib=28, far=()
):
    def kernel(*refs):
        lead = len(scalars) + len(ins)
        sources, rest = refs[:lead], refs[lead + dep_count :]
        targets, rest = list(rest[: len(outs)]), rest[len(outs) :]
        stages, rest = rest[: len(far)], rest[len(far) :]
        copies = []
        for place, (index, stage) in enumerate(zip(far, stages)):
            copies.append(pltpu.make_async_copy(stage, targets[index], rest[-1].at[place]))
            targets[index] = stage
        body(*sources, *targets, *(rest[:-1] if far else rest))
        for copy in copies:
            copy.start()
        for copy in copies:
            copy.wait()

    def spec(shape):
        rank = len(shape)
        return pl.BlockSpec(shape, lambda i: (0,) * rank, pipeline_mode=pl.Buffered(1))

    def out_spec(index, shape):
        if index in far:
            return pl.BlockSpec(memory_space=pltpu.HBM)
        if shape == (1,):
            return pl.BlockSpec(memory_space=pltpu.SMEM)
        return spec(shape)

    scratch = [pltpu.VMEM(*outs[index]) for index in far] + list(scratch)
    if far:
        scratch.append(pltpu.SemaphoreType.DMA((len(far),)))
    dep_count = 0

    def build(deps):
        nonlocal dep_count
        dep_count = len(deps)
        return pl.pallas_call(
            kernel,
            grid=(1,),
            out_shape=tuple(jax.ShapeDtypeStruct(shape, kind) for shape, kind in outs),
            in_specs=[pl.BlockSpec(memory_space=pltpu.SMEM)] * len(scalars)
            + [spec(a.shape) for a in ins]
            + [pl.BlockSpec(memory_space=pl.ANY)] * len(deps),
            out_specs=tuple(out_spec(index, shape) for index, (shape, _) in enumerate(outs)),
            scratch_shapes=scratch,
            compiler_params=pltpu.CompilerParams(vmem_limit_bytes=mib << 20),
            cost_estimate=LIGHT,
            name=name,
        )(*scalars, *ins, *deps)

    result = in_order(name, deps, ins, build)
    return result[0] if len(outs) == 1 else result


def ring_send(ahead, behind):
    return ring_pass(ahead, 1), ring_pass(behind, -1)


def copy_body(*refs):
    count = len(refs) // 2
    for source, target in zip(refs[:count], refs[count:]):
        target[...] = source[...]


def relay(*arrays, deps=()):
    result = call("relay", copy_body, [(a.shape, a.dtype) for a in arrays], arrays, deps=deps)
    return result if len(arrays) > 1 else [result]


class Gather:
    def __init__(self, shard):
        self.pieces = [shard]
        self.ring = lax.axis_size("dp") == 8
        if self.ring:
            self.send(shard, shard)
        else:
            self.pieces = [lax.all_gather(shard, "dp", axis=0, tiled=True)]

    def send(self, ahead, behind):
        self.got = ring_send(ahead, behind)
        self.pieces += self.got

    def forward(self):
        if self.ring:
            self.send(*self.got)

    def relay(self, deps=()):
        if self.ring:
            self.send(*relay(*self.got, deps=deps))

    def halve(self):
        if not self.ring:
            return
        rows, columns = self.pieces[0].shape
        half = rows // 2

        def body(ahead, behind, upper, lower):
            upper[...] = ahead[pl.ds(0, half), :]
            lower[...] = behind[pl.ds(half, half), :]

        self.send(*call("halve", body, [((half, columns), BF)] * 2, self.got))

    def place(self, place, width):
        if not self.ring:
            return self.pieces[0]

        def body(place, *refs):
            put_pieces(place, refs[:-1], refs[-1])

        shape = (width, self.pieces[0].shape[1])
        return call("place_shards", body, [(shape, BF)], self.pieces, [place])


def put_pieces(place, pieces, full):
    if len(pieces) == 1:
        full[...] = pieces[0][...]
        return
    rows = pieces[0].shape[0]
    half = rows // 2
    whole_pieces = len(pieces) - 2
    for index, piece in enumerate(pieces):
        owner = place[1 + min(index, whole_pieces)]
        start = owner * rows + max(index - whole_pieces, 0) * half
        full[pl.ds(pl.multiple_of(start, half), piece.shape[0]), :] = piece[...]


def ring_kernel(name, body, outs, place, partial, picks, ins=(), scalars=(), deps=()):
    rows, columns = outs[0][0][0], partial.shape[1]
    if not picks or partial.shape[0] == rows:
        picks, block_rows = picks or (0,), partial.shape[0]
        blocks = [pl.BlockSpec((block_rows, columns), lambda i, s: (0, 0))] * len(picks)
    else:
        block_rows = partial.shape[0] // lax.axis_size("dp")
        blocks = [
            pl.BlockSpec((block_rows, columns), functools.partial(pick_block, 1 + OFFSETS.index(o)))
            for o in picks
        ]

    def kernel(_, *refs):
        lead = len(scalars) + len(picks) + len(ins)
        body(*refs[:lead], *refs[lead + dep_count :])

    dep_count = 0

    def fixed(shape):
        if shape == (1,):
            return pl.BlockSpec(memory_space=pltpu.SMEM)
        return pl.BlockSpec(shape, lambda i, s: (0, 0))

    def build(deps):
        nonlocal dep_count
        dep_count = len(deps)
        return pl.pallas_call(
            kernel,
            grid_spec=pltpu.PrefetchScalarGridSpec(
                num_scalar_prefetch=1,
                grid=(1,),
                in_specs=[pl.BlockSpec(memory_space=pltpu.SMEM)] * len(scalars)
                + blocks
                + [fixed(a.shape) for a in ins]
                + [pl.BlockSpec(memory_space=pl.ANY)] * len(deps),
                out_specs=tuple(fixed(shape) for shape, _ in outs),
            ),
            out_shape=tuple(jax.ShapeDtypeStruct(shape, kind) for shape, kind in outs),
            compiler_params=pltpu.CompilerParams(vmem_limit_bytes=24 << 20),
            cost_estimate=LIGHT,
            name=name,
        )(place, *scalars, *[partial] * len(picks), *ins, *deps)

    return in_order(name, deps, (partial, *ins), build)


def pick_block(column, i, place):
    return (place[column], 0)


def far_body(block, upper, lower):
    half = upper.shape[0]
    upper[...] = block[pl.ds(0, half), :]
    lower[...] = block[pl.ds(half, half), :]


def half_step_body(more, less, ahead, behind, more_out, less_out):
    half = ahead.shape[0]
    upper, lower = pl.ds(0, half), pl.ds(half, half)
    more_out[upper, :] = (more[upper, :].astype(F32) + ahead[...].astype(F32)).astype(BF)
    more_out[lower, :] = more[lower, :]
    less_out[upper, :] = less[upper, :]
    less_out[lower, :] = (less[lower, :].astype(F32) + behind[...].astype(F32)).astype(BF)


def step_body(more, less, ahead, behind, more_out, less_out):
    more_out[...] = (more[...].astype(F32) + ahead[...].astype(F32)).astype(BF)
    less_out[...] = (less[...].astype(F32) + behind[...].astype(F32)).astype(BF)


class Scatter:
    def __init__(self, partial, place, deps=()):
        self.count = lax.axis_size("dp")
        self.partial, self.place = partial, place
        self.offset = 4
        if self.count != 8:
            total = lax.psum_scatter(partial, "dp", scatter_dimension=0, tiled=True)
            self.terms = [total, jnp.zeros_like(total), jnp.zeros_like(total)]
            self.got = ()
            return
        self.rows, self.columns = partial.shape[0] // self.count, partial.shape[1]
        self.run("scatter_first", far_body, self.rows // 2, (4,), (), deps)

    def run(self, name, body, rows, picks, arrived, deps=()):
        outs = [((rows, self.columns), BF)] * 2
        sends = ring_kernel(
            name, body, outs, self.place, self.partial, picks, arrived, deps=deps
        )
        self.got = ring_send(*sends)
        self.offset -= 1
        self.terms = [self.partial, *self.got]

    def step(self, deps=()):
        if self.count == 8:
            body = half_step_body if self.offset == 3 else step_body
            picks = (self.offset, -self.offset)
            self.run("scatter_step", body, self.rows, picks, self.got, deps)


def sum_body_two(left, right, out):
    out[...] = left[...] + right[...]


def sum_over_dp(value):
    distance = 1
    while distance < lax.axis_size("dp"):
        pairs = [(i, i ^ distance) for i in range(lax.axis_size("dp"))]
        other = lax.ppermute(value, "dp", pairs)
        value = call("norm_sum", sum_body_two, [(value.shape, F32)], [value, other])
        distance *= 2
    return value


def turn(upper, lower, cosine, sine):
    return upper * cosine - lower * sine, lower * cosine + upper * sine


def key_blocks(block):
    return max(block + 1, PREFIX_MAX // BLOCK)


def visible_keys(block, other, prefix):
    if other < block:
        return None
    keys = other * BLOCK + lax.broadcasted_iota(jnp.int32, (BLOCK, BLOCK), 0)
    queries = block * BLOCK + lax.broadcasted_iota(jnp.int32, (BLOCK, BLOCK), 1)
    return (keys <= queries) | (keys < prefix)


def lanes(index, size=BLOCK):
    return pl.ds(pl.multiple_of(index * size, size), size)


def query_blocks(group, side, work):
    for chip in range(TENSOR // 2):

        @pl.when(((group >> 1) ^ side) == chip)
        def _():
            for block in (2 * chip, 2 * chip + 1):
                work(block, (block ^ group) & 1)


def attend(group, prefix, side, q, k_rows, v, o_out, lse_out):
    def work(block, slot):
        here, target = pl.ds(block * BLOCK, BLOCK), lanes(slot)

        @pl.loop(0, GROUP)
        def _(head):
            own = jnp.where(head + group >= SHARE, 1, 0)
            query = q[lanes(head, HD), here]
            scores = []
            for other in range(key_blocks(block)):
                raw = dot(k_rows[own, pl.ds(other * BLOCK, BLOCK), :], query, 1, 0)
                mask = visible_keys(block, other, prefix)
                scores.append(raw if mask is None else jnp.where(mask, raw, MASKED))
            highest = jnp.max(functools.reduce(jnp.maximum, scores), axis=0, keepdims=True)
            total = jnp.zeros((1, BLOCK), F32)
            attended = jnp.zeros((HD, BLOCK), F32)
            for other, score in enumerate(scores):
                weight = jnp.exp(score - highest)
                total += jnp.sum(weight, axis=0, keepdims=True)
                attended += dot(
                    v[lanes(own, HD), pl.ds(other * BLOCK, BLOCK)], weight.astype(BF), 1, 0
                )
            o_out[lanes(head, HD), target] = (attended / total).astype(BF)
            lse_out[pl.ds(head, 1), target] = highest + jnp.log(total)

    query_blocks(group, side, work)


def project_out(o, weight, outs):
    for slot, out in enumerate(outs):
        out[...] = dot(o[:, pl.ds(slot * BLOCK, BLOCK)], weight[...], 0, 1).astype(BF)


def front_body(count, place, prefix, *refs):
    pieces, refs = refs[:count], refs[count:]
    tokens, refs = refs[:TENSOR], refs[TENSOR:]
    cosine, sine, full, out_w, gains, rows_one, inv_rows, q, k, v, k_rows, v_rows = refs[:12]
    o_out, lse_out, keep, send = refs[12:]
    group = place[0]
    half = HD // 2
    put_pieces(place, pieces, full)
    out_w[...] = full[:, pl.ds(KV_COLS + Q_COLS + GAIN_COLS, Q_COLS)]
    qkv_w = full[:, pl.ds(0, KV_COLS + Q_COLS)]
    gain_rows = full[:, pl.ds(KV_COLS + Q_COLS, GAIN_COLS)].astype(F32).T[:8]
    gains[...] = gain_rows
    for index in range(TENSOR):
        rows = pl.ds(index * BLOCK, BLOCK)
        values = tokens[index][...].astype(F32)
        inv = inverse_root(values)
        inv_rows[rows, :] = inv
        normed = (values * inv * gain_rows[:1]).astype(BF)
        rows_one[rows, :] = normed
        flat = dot(normed, qkv_w, 1, 0)
        block = index ^ group
        here = lanes(block)
        cos, sin = cosine[:, here], sine[:, here]
        turned = flat.T
        for head in range(PAIR + GROUP):
            row = head * HD if head < PAIR else KV_COLS + (head - PAIR) * HD
            upper, lower = turn(turned[row : row + half], turned[row + half : row + HD], cos, sin)
            both = jnp.concatenate([upper, lower], axis=0)
            if head < PAIR:
                k[pl.ds(row, HD), here] = both.astype(BF)
                k_rows[head, here, :] = both.T.astype(BF)
            else:
                scaled = both.astype(BF) * jnp.asarray(HD**-0.5, BF)
                q[pl.ds(row - KV_COLS, HD), here] = scaled
        v[:, here] = turned[PAIR * HD : KV_COLS].astype(BF)
        for head in range(PAIR):
            start = (PAIR + head) * HD
            v_rows[head, here, :] = flat[:, start : start + HD].astype(BF)
    attend(group, prefix[0], 1, q, k_rows, v, o_out, lse_out)
    project_out(o_out, out_w, (keep, send))


def near_body(place, prefix, q, k_rows, v, out_w, o_out, lse_out, keep, send):
    attend(place[0], prefix[0], 0, q, k_rows, v, o_out, lse_out)
    project_out(o_out, out_w, (keep, send))


def attend_back(side, place, prefix, mixed, out_w, q, k, k_rows, v_rows, o, lse, cosine, sine, dq, dk, dv, grad):
    group, prefix = place[0], prefix[0]
    half = HD // 2
    for slot in range(2):
        grad[:, pl.ds(slot * BLOCK, BLOCK)] = dot(mixed[slot][...], out_w[...], 1, 0).T.astype(BF)

    def work(block, slot):
        here, target = pl.ds(block * BLOCK, BLOCK), lanes(slot)

        @pl.loop(0, GROUP)
        def _(head):
            own = jnp.where(head + group >= SHARE, 1, 0)
            rows = lanes(head, HD)
            query = q[rows, here]
            grad_here = grad[rows, target]
            inner = jnp.sum(
                grad_here.astype(F32) * o[rows, target].astype(F32), axis=0, keepdims=True
            )
            logs = lse[pl.ds(head, 1), target]
            total = jnp.zeros((HD, BLOCK), F32)
            for other in range(key_blocks(block)):
                there = pl.ds(other * BLOCK, BLOCK)
                probs = jnp.exp(dot(k_rows[own, there, :], query, 1, 0) - logs)
                mask = visible_keys(block, other, prefix)
                if mask is not None:
                    probs = jnp.where(mask, probs, 0.0)
                prob_grad = dot(v_rows[own, there, :], grad_here, 1, 0)
                score_grad = (probs * (prob_grad - inner)).astype(BF)
                total += dot(k[lanes(own, HD), there], score_grad, 1, 0)
                dk[own, there, :] += dot(score_grad, query, 1, 1)
                dv[own, there, :] += dot(probs.astype(BF), grad_here, 1, 1)
            total = total * HD**-0.5
            upper, lower = turn(total[:half], total[half:], cosine[:, here], -sine[:, here])
            dq[rows, target] = jnp.concatenate([upper, lower], axis=0).astype(BF)

    query_blocks(group, side, work)


def back_near_body(place, prefix, m0, m1, out_w, q, k, k_rows, v_rows, o, lse, cosine, sine, dq, dk, dv, grad):
    dk[...] = jnp.zeros_like(dk)
    dv[...] = jnp.zeros_like(dv)
    attend_back(
        0, place, prefix, (m0, m1), out_w, q, k, k_rows, v_rows, o, lse, cosine, sine, dq, dk, dv, grad
    )


def back_far_body(
    place, prefix, m0, m1, out_w, q, k, k_rows, v_rows, o, lse, cosine, sine, dk_in, dv_in, dq, dkv, dk, dv, grad
):
    half = HD // 2
    dk[...] = dk_in[...]
    dv[...] = dv_in[...]
    attend_back(
        1, place, prefix, (m0, m1), out_w, q, k, k_rows, v_rows, o, lse, cosine, sine, dq, dk, dv, grad
    )
    for block in range(TENSOR):
        here, target = pl.ds(block * BLOCK, BLOCK), lanes(block ^ place[0])
        for head in range(PAIR):
            turned = dk[head, here, :].T
            upper, lower = turn(turned[:half], turned[half:], cosine[:, here], -sine[:, here])
            dkv[pl.ds(head * HD, HD), target] = jnp.concatenate([upper, lower], axis=0).astype(BF)
            dkv[pl.ds((PAIR + head) * HD, HD), target] = dv[head, here, :].T.astype(BF)


def norm_body(tokens, keep, near, far, gains, mixed, normed):
    values = tokens[...].astype(F32) + (
        (keep[...].astype(F32) + near[...].astype(F32)) + far[...].astype(F32)
    )
    mixed[...] = values
    normed[...] = (values * inverse_root(values) * gains[1:2]).astype(BF)


def norm_back_body(keep, near, far, mixed, cotangent, gains, grad, grad_low, gain_grad):
    normed_grad = (keep[...].astype(F32) + near[...].astype(F32)) + far[...].astype(F32)
    values = mixed[...]
    inv = inverse_root(values)
    hat = values * inv
    gain_grad[...] = jnp.broadcast_to(
        jnp.sum(normed_grad * hat, axis=0, keepdims=True), gain_grad.shape
    )
    total = cotangent[...].astype(F32) + norm_back(normed_grad, hat, inv, gains[1:2])
    grad[...] = total
    grad_low[...] = total.astype(BF)


def input_grad_body(keep, nears, far, tokens, mixed_grad, gains, out):
    near = nears[pl.ds(0, BLOCK), :].astype(F32)
    normed_grad = (keep[...].astype(F32) + near) + far[...].astype(F32)
    values = tokens[...].astype(F32)
    inv = inverse_root(values)
    out[...] = mixed_grad[...] + norm_back(normed_grad, values * inv, inv, gains[0:1])


def output_body(keep, near, far, mixed, out):
    out[...] = (
        mixed[...] + ((keep[...].astype(F32) + near[...].astype(F32)) + far[...].astype(F32))
    ).astype(BF)


def add_second_body(left, rights, out):
    right = rights[pl.ds(BLOCK, BLOCK), :]
    out[...] = (left[...].astype(F32) + right.astype(F32)).astype(BF)


def add_body(left, right, out):
    out[...] = (left[...].astype(F32) + right[...].astype(F32)).astype(BF)


def hidden_body(a0, a1, weight, by_gate, by_up, hidden):
    columns = hidden.shape[1]
    for slot, rows in enumerate((a0, a1)):
        both = dot(rows[...], weight[:, pl.ds(0, 2 * columns)], 1, 0)
        gate, up = both[:, :columns], both[:, columns:]
        sigma = jax.nn.sigmoid(gate)
        silu = gate * sigma
        here = pl.ds(slot * BLOCK, BLOCK)
        by_gate[here, :] = (up * sigma * (1.0 + gate * (1.0 - sigma))).astype(BF)
        by_up[here, :] = silu.astype(BF)
        hidden[here, :] = (silu * up).astype(BF)


def hidden_back_body(c0, c1, weight, by_gate, by_up, grads, part0, part1):
    columns = by_gate.shape[1]
    for slot, (rows, part) in enumerate(((c0, part0), (c1, part1))):
        here = pl.ds(slot * BLOCK, BLOCK)
        grad = dot(rows[...], weight[:, pl.ds(2 * columns, columns)], 1, 0)
        grads[here, pl.ds(0, columns)] = (grad * by_gate[here, :].astype(F32)).astype(BF)
        grads[here, pl.ds(columns, columns)] = (grad * by_up[here, :].astype(F32)).astype(BF)
        part[...] = dot(grads[here, :], weight[:, pl.ds(0, 2 * columns)], 1, 1).astype(BF)


def down_body(near, far, weight, *parts):
    columns = near.shape[1]
    down = weight[:, pl.ds(2 * columns, columns)]
    for index, part in enumerate(parts):
        source = (near, far)[index // 2]
        part[...] = dot(source[pl.ds(index % 2 * BLOCK, BLOCK), :], down, 1, 1).astype(BF)


def column_grad(lefts, rights):
    width, columns = lefts[0].shape[1], rights[0].shape[1]
    tile = 256

    def kernel(*refs):
        left = jnp.concatenate([ref[...] for ref in refs[:TENSOR]], axis=0)
        right = jnp.concatenate([ref[...] for ref in refs[TENSOR : TENSOR + 2]], axis=0)
        refs[-1][...] = dot(left, right, 0, 0).astype(BF)

    length = TENSOR * BLOCK

    def build(deps):
        return pl.pallas_call(
            kernel,
            grid=(width // tile,),
            out_shape=(jax.ShapeDtypeStruct((width, columns), BF),),
            in_specs=[pl.BlockSpec((BLOCK, tile), lambda i: (0, i))] * TENSOR
            + [pl.BlockSpec(right.shape, lambda i: (0, 0)) for right in rights]
            + [pl.BlockSpec(memory_space=pl.ANY)] * len(deps),
            out_specs=(pl.BlockSpec((tile, columns), lambda i: (i, 0)),),
            compiler_params=pltpu.CompilerParams(vmem_limit_bytes=28 << 20),
            cost_estimate=LIGHT,
            name="column_grad",
        )(*lefts, *rights, *deps)

    return in_order("column_grad", (), (*lefts, *rights), build)[0]


def last_grad_kernel(rows_one, *refs):
    mixed, refs = refs[:TENSOR], refs[TENSOR:]
    tokens, refs = refs[:TENSOR], refs[TENSOR:]
    inv_rows, weight, dkv, dq_near, dq_far, o_near, o_far, gain_two = refs[:8]
    keep, far_keep, sends, out = refs[-4:]
    tile = rows_one.shape[1]
    grads = jnp.concatenate(
        [dkv[...], jnp.concatenate([dq_near[...], dq_far[...]], axis=1)], axis=0
    )
    spread = dot(weight[:, pl.ds(0, KV_COLS + Q_COLS)], grads, 1, 0).T
    gain_one = jnp.zeros((1, tile), F32)
    for index in range(TENSOR):
        here = slice(index * BLOCK, (index + 1) * BLOCK)
        block = spread[here]
        if index % 2:
            sends[pl.ds(index // 2 * BLOCK, BLOCK), :] = block.astype(BF)
        else:
            (keep, far_keep)[index // 2][...] = block.astype(BF)
        hat = tokens[index][...].astype(F32) * inv_rows[here, :]
        gain_one += jnp.sum(block * hat, axis=0, keepdims=True)
    rows = jnp.concatenate(
        [
            dot(grads, rows_one[...], 1, 0),
            gain_one,
            gain_two[0:1],
            jnp.zeros((GAIN_COLS - 2, tile), F32),
        ],
        axis=0,
    )
    columns = rows.shape[0]
    out[:, pl.ds(0, columns)] = rows.T.astype(BF)
    attended = jnp.concatenate([o_near[...], o_far[...]], axis=1)
    mixed_all = jnp.concatenate([block[...] for block in mixed], axis=0)
    out[:, pl.ds(columns, Q_COLS)] = dot(attended, mixed_all, 1, 0).T.astype(BF)


def last_grad(rows_one, mixed, tokens, inv_rows, weight, dkv, dq, o, gain_two, deps):
    length, width = rows_one.shape
    columns = KV_COLS + Q_COLS + GAIN_COLS + Q_COLS
    tile = 256
    by_block = pl.BlockSpec((BLOCK, tile), lambda i: (0, i))

    def fixed(array):
        return pl.BlockSpec(array.shape, lambda i: (0, 0))

    operands = (rows_one, *mixed, *tokens, inv_rows, weight, dkv, *dq, *o, gain_two)

    def build(deps):
        return pl.pallas_call(
            last_grad_kernel,
            grid=(width // tile,),
            out_shape=tuple(
                jax.ShapeDtypeStruct((c, width), BF) for c in (BLOCK, BLOCK, 2 * BLOCK)
            )
            + (jax.ShapeDtypeStruct((width, columns), BF),),
            in_specs=[pl.BlockSpec((length, tile), lambda i: (0, i))]
            + [by_block] * (2 * TENSOR)
            + [
                fixed(inv_rows),
                pl.BlockSpec((tile, weight.shape[1]), lambda i: (i, 0)),
                fixed(dkv),
                *(fixed(array) for array in (*dq, *o)),
                pl.BlockSpec((8, tile), lambda i: (0, i)),
            ]
            + [pl.BlockSpec(memory_space=pl.ANY)] * len(deps),
            out_specs=(by_block, by_block, pl.BlockSpec((2 * BLOCK, tile), lambda i: (0, i)))
            + (pl.BlockSpec((tile, columns), lambda i: (i, 0)),),
            compiler_params=pltpu.CompilerParams(vmem_limit_bytes=32 << 20),
            cost_estimate=LIGHT,
            name="last_grad",
        )(*operands, *deps)

    return in_order("last_grad", deps, operands, build)


def cast_first_body(place, keyval, query, outproj, gains, out):
    for index in range(2):
        start = index * KV * HD
        chosen = keyval[:, pl.ds(start, PAIR * HD)]
        for group in range(1, TENSOR):
            chosen = jnp.where(
                place[0] == group, keyval[:, pl.ds(start + group * HD, PAIR * HD)], chosen
            )
        out[:, pl.ds(index * PAIR * HD, PAIR * HD)] = chosen.astype(BF)
    rows = gains.shape[1]
    filled = jnp.concatenate([gains[...], jnp.zeros((GAIN_COLS - 2, rows), F32)], axis=0)
    out[:, pl.ds(KV_COLS, Q_COLS + GAIN_COLS)] = jnp.concatenate(
        [query[...], filled.T], axis=1
    ).astype(BF)
    out[:, pl.ds(KV_COLS + Q_COLS + GAIN_COLS, Q_COLS)] = outproj[...].astype(BF)


def cast_mlp_body(gate_up, down, out):
    columns = down.shape[1]
    for index, source in enumerate((gate_up[0], gate_up[1], down[...])):
        out[:, pl.ds(index * columns, columns)] = source.astype(BF)


def cast_body(weight, out):
    out[...] = weight[...].astype(BF)


def sum_body(block, ahead, behind, total, squares):
    values = block[...].astype(F32) + (ahead[...].astype(F32) + behind[...].astype(F32))
    total[...] = values
    squares[0] = jnp.sum(values * values)


def pack_body(gate_up_squares, down_squares, block, ahead, behind, total, shared):
    values = block[...].astype(F32) + (ahead[...].astype(F32) + behind[...].astype(F32))
    total[...] = values
    query = values[:, KV_COLS : KV_COLS + Q_COLS]
    outproj = values[:, KV_COLS + Q_COLS + GAIN_COLS :]
    own = jnp.sum(query * query, axis=0, keepdims=True)
    own = jnp.sum(own + jnp.sum(outproj * outproj, axis=0, keepdims=True), axis=1, keepdims=True)
    own = own + (gate_up_squares[0] + down_squares[0])
    first = own.astype(BF).astype(F32)
    second = (own - first).astype(BF).astype(F32)
    third = (own - first - second).astype(BF).astype(F32)
    gains = values[:, KV_COLS + Q_COLS : KV_COLS + Q_COLS + GAIN_COLS]
    lane = lax.broadcasted_iota(jnp.int32, gains.shape, 1)
    for index, part in enumerate((first, second, third)):
        gains = jnp.where(lane == 2 + index, part, gains)
    shared[...] = jnp.concatenate([values[:, :KV_COLS], gains], axis=1).astype(BF)


def shared_body(place, own, near, far, far_near, keyval, gains, squares, by_index):
    for index, piece in enumerate((own, near, far, far_near)):
        by_index[index ^ place[0]] = piece[...].astype(F32)
    gains_sum = functools.reduce(
        jnp.add, [by_index[index, :, pl.ds(KV_COLS, GAIN_COLS)] for index in range(TENSOR)]
    )
    rows = gains_sum.T[:8]
    gains[...] = rows
    heads = []
    for start in (0, PAIR * HD):
        for head in range(KV):
            readers = []
            if head < TENSOR:
                readers.append(by_index[head, :, pl.ds(start, HD)])
            if head > 0:
                readers.append(by_index[head - 1, :, pl.ds(start + HD, HD)])
            heads.append(sum(readers[1:], readers[0]))
    total = jnp.concatenate(heads, axis=1)
    keyval[...] = total
    squares[...] = jnp.full(
        squares.shape,
        jnp.sum(total * total) + jnp.sum(rows[:2] * rows[:2]) + jnp.sum(rows[2:5, :1]),
    )


def hold_body(*refs):
    count = (len(refs) - 1) // 2
    copies = [
        pltpu.make_async_copy(refs[index], refs[count + index], refs[-1].at[index])
        for index in range(count)
    ]
    for copy in copies:
        copy.start()
    for copy in copies:
        copy.wait()


def hold(arrays):
    dep_count = 0

    def kernel(*refs):
        hold_body(*refs[: len(arrays)], *refs[len(arrays) + dep_count :])

    def build(deps):
        nonlocal dep_count
        dep_count = len(deps)
        return pl.pallas_call(
            kernel,
            out_shape=tuple(jax.ShapeDtypeStruct(array.shape, array.dtype) for array in arrays),
            in_specs=[pl.BlockSpec(memory_space=pltpu.HBM)] * len(arrays)
            + [pl.BlockSpec(memory_space=pl.ANY)] * len(deps),
            out_specs=tuple([pl.BlockSpec(memory_space=pltpu.VMEM)] * len(arrays)),
            scratch_shapes=[pltpu.SemaphoreType.DMA((len(arrays),))],
            compiler_params=pltpu.CompilerParams(vmem_limit_bytes=52 << 20),
            cost_estimate=LIGHT,
            name="hold",
        )(*arrays, *deps)

    return in_order("hold", (), arrays, build)


def adam_kernel(limit, total, gains_grad, gains, gains_first, gains_second, *refs):
    count = 5
    keyval_grad, last_grad, gate_up_grad, down_grad = refs[:4]
    weights, outs = refs[4 : 4 + 3 * count], refs[4 + 3 * count :]
    norm = jnp.sqrt(total[...])
    clip = limit / jnp.maximum(norm[0:1, 0:1], limit)
    outs[-1][0] = jnp.max(norm)
    gains_out = outs[3 * count : 3 * count + 3]
    gains_out[0][...], gains_out[1][...], gains_out[2][...] = adam_step(
        gains[...], gains_first[...], gains_second[...], gains_grad[0:2], 0.25, clip
    )
    tile = keyval_grad.shape[0]
    here = pl.ds(0, tile)
    if weights[0].shape[0] > tile:
        here = pl.ds(pl.multiple_of(pl.program_id(0) * tile, tile), tile)
    hidden = down_grad.shape[1]
    out_start = KV_COLS + Q_COLS + GAIN_COLS
    grads = (
        last_grad[:, pl.ds(KV_COLS, Q_COLS)],
        keyval_grad[...],
        last_grad[:, pl.ds(out_start, Q_COLS)],
        None,
        down_grad[...],
    )
    rates = (
        0.5 / math.sqrt(D),
        0.5 / math.sqrt(D),
        2.0 / math.sqrt(HEADS * HD),
        0.5 / math.sqrt(D),
        0.5 / math.sqrt(FF),
    )
    for index in range(count):
        held = weights[3 * index : 3 * index + 3]
        first_new, second_new, weight_new = outs[3 * index : 3 * index + 3]
        if grads[index] is None:
            for side in range(2):
                first_new[side], second_new[side], weight_new[side] = adam_step(
                    *(ref[side, here, :] for ref in held),
                    gate_up_grad[:, pl.ds(side * hidden, hidden)],
                    rates[index],
                    clip,
                )
        else:
            first_new[...], second_new[...], weight_new[...] = adam_step(
                *(ref[here, :] for ref in held), grads[index], rates[index], clip
            )


def adam_all(limit, total, gains_grad, gains, grads, weights):
    rows = grads[0].shape[0]
    tile = 32 if rows % 32 == 0 else rows

    def spec(array):
        if array.ndim == 3:
            return pl.BlockSpec((2, tile, array.shape[2]), lambda i: (0, i, 0))
        return pl.BlockSpec((tile, array.shape[1]), lambda i: (i, 0))

    def fixed(array):
        return pl.BlockSpec(array.shape, lambda i: (0, 0))

    return pl.pallas_call(
        functools.partial(adam_kernel, limit),
        grid=(rows // tile,),
        out_shape=tuple(jax.ShapeDtypeStruct(array.shape, F32) for array in (*weights, *gains))
        + (jax.ShapeDtypeStruct((1,), F32),),
        in_specs=[fixed(array) for array in (total, gains_grad, *gains)]
        + [spec(array) for array in grads]
        + [pl.BlockSpec(memory_space=pltpu.VMEM)] * len(weights),
        out_specs=tuple(spec(array) for array in weights)
        + tuple(fixed(array) for array in gains)
        + (pl.BlockSpec(memory_space=pltpu.SMEM),),
        compiler_params=pltpu.CompilerParams(vmem_limit_bytes=24 << 20),
        cost_estimate=LIGHT,
        name="adam_all",
    )(total, gains_grad, *gains, *grads, *weights)


def per_device(
    tokens,
    prefix,
    cotangent,
    query_weight,
    query_first,
    query_second,
    keyval_weight,
    keyval_first,
    keyval_second,
    outproj_weight,
    outproj_first,
    outproj_second,
    gate_up_weight,
    gate_up_first,
    gate_up_second,
    down_weight,
    down_first,
    down_second,
    norm_gains,
    gains_first,
    gains_second,
):
    replica_count = lax.axis_size("dp")
    rows_local, width = tokens.shape[1:]
    length = rows_local * TENSOR
    share, query_columns = query_weight.shape
    hidden = gate_up_weight.shape[2]
    assert tokens.shape[0] == 1 and lax.axis_size("tensor") == TENSOR
    assert rows_local == BLOCK and query_columns == Q_COLS
    TRAIL[0] = None
    place = lax.dynamic_index_in_dim(
        jnp.asarray(place_table(replica_count)), lax.axis_index(("dp", "tensor")), 0, False
    )
    cosine, sine = (jnp.asarray(table) for table in rope_tables(length))
    tokens, cotangent = tokens[0], cotangent[0]
    block_low, block_float = ((BLOCK, width), BF), ((BLOCK, width), F32)
    half_length = 2 * BLOCK

    first_columns = KV_COLS + 2 * Q_COLS + GAIN_COLS
    first = Gather(
        call(
            "cast_first",
            cast_first_body,
            [((share, first_columns), BF)],
            [keyval_weight, query_weight, outproj_weight.T, norm_gains],
            [place],
            mib=56,
        )
    )
    (token_low,) = relay(tokens)
    token_near, token_far = swap(token_low, 1), swap(token_low, 2)
    first.forward()
    first.forward()
    token_blocks = [
        token_low,
        token_near,
        token_far,
        swap(relay(token_far, deps=first.pieces[3:5])[0], 1),
    ]
    (cot_low,) = relay(cotangent)
    cot_near, cot_far = swap(cot_low, 1), swap(cot_low, 2)
    first.halve()
    cot_blocks = [cot_low, cot_near, cot_far, swap(relay(cot_far)[0], 1)]
    second = Gather(
        call(
            "cast_mlp",
            cast_mlp_body,
            [((share, 3 * hidden), BF)],
            [gate_up_weight, down_weight.T],
            deps=first.pieces[-2:],
        )
    )

    heads_low = ((Q_COLS, half_length), BF)
    logs = ((8, half_length), F32)
    (
        first_full,
        out_full,
        gains,
        rows_one,
        inv_rows,
        q,
        k,
        v,
        k_rows,
        v_rows,
        o_far,
        lse_far,
        far_keep,
        far_send,
    ) = call(
        "front",
        functools.partial(front_body, len(first.pieces)),
        [
            ((width, first_columns), BF),
            ((width, Q_COLS), BF),
            ((8, width), F32),
            ((length, width), BF),
            ((length, 1), F32),
            ((Q_COLS, length), BF),
            ((PAIR * HD, length), BF),
            ((PAIR * HD, length), BF),
            ((PAIR, length, HD), BF),
            ((PAIR, length, HD), BF),
            heads_low,
            logs,
            block_low,
            block_low,
        ],
        [*first.pieces, *token_blocks, cosine, sine],
        [place, prefix],
        mib=32,
        far=(0, 3),
    )
    far_sum = call("far_sum", add_body, [block_low], [far_keep, swap(far_send, 1)])
    attn_far = swap(far_sum, 2)
    second.relay()
    o_near, lse_near, near_keep, near_send = call(
        "near",
        near_body,
        [heads_low, logs, block_low, block_low],
        [q, k_rows, v, out_full],
        [place, prefix],
        deps=[cot_near, cot_blocks[3]],
    )
    near_got = swap(near_send, 1)
    second.relay([attn_far])
    mixed_one, rows_two = call(
        "norm",
        norm_body,
        [block_float, block_low],
        [tokens, near_keep, near_got, attn_far, gains],
        far=(0,),
    )
    two_near, two_far = swap(rows_two, 1), swap(rows_two, 2)
    a2 = [rows_two, two_near, two_far, swap(relay(two_far)[0], 1)]
    second.halve()
    mlp_full = second.place(place, width)
    mlp_out = [((half_length, hidden), BF)] * 3
    gate_near, up_near, hidden_near = call(
        "hidden_near", hidden_body, mlp_out, [rows_two, two_near, mlp_full]
    )
    gate_far, up_far, hidden_far = call(
        "hidden_far", hidden_body, mlp_out, [a2[2], a2[3], mlp_full]
    )
    down_grad = column_grad(cot_blocks, [hidden_near, hidden_far])
    down_ring = Scatter(down_grad, place)
    back_out = [((half_length, 2 * hidden), BF), block_low, block_low]
    grads_far, far_keep, far_send = call(
        "hidden_back_far",
        hidden_back_body,
        back_out,
        [cot_blocks[2], cot_blocks[3], mlp_full, gate_far, up_far],
    )
    far_got = swap(far_send, 1)
    down_ring.step()
    far_sum = call("far_sum", add_body, [block_low], [far_keep, far_got])
    part_far = swap(far_sum, 2)
    grads_near, near_keep, near_send = call(
        "hidden_back_near",
        hidden_back_body,
        back_out,
        [cot_blocks[0], cot_blocks[1], mlp_full, gate_near, up_near],
    )
    near_got = swap(near_send, 1)
    gate_up_grad = column_grad(a2, [grads_near, grads_far])
    down_ring.step()
    gate_up_ring = Scatter(gate_up_grad, place, [part_far])
    mixed_grad, mixed_low, gain_two = call(
        "norm_back",
        norm_back_body,
        [block_float, block_low, ((8, width), F32)],
        [near_keep, near_got, part_far, mixed_one, cotangent, gains],
        far=(0,),
    )
    mixed_near, mixed_far = swap(mixed_low, 1), swap(mixed_low, 2)
    sums = [((PAIR, length, HD), F32)] * 2
    held = [pltpu.VMEM((Q_COLS, half_length), BF)]
    dq_near, dk, dv = call(
        "attention_back_near",
        back_near_body,
        [heads_low, *sums],
        [mixed_low, mixed_near, out_full, q, k, k_rows, v_rows, o_near, lse_near, cosine, sine],
        [place, prefix],
        scratch=held,
    )
    gate_up_ring.step()
    down_ring.step()
    mixed = [mixed_low, mixed_near, mixed_far, swap(relay(mixed_far)[0], 1)]
    parts = call(
        "down_part",
        down_body,
        [block_low] * TENSOR,
        [hidden_near, hidden_far, mlp_full],
    )
    out_got = [swap(parts[1], 1), swap(parts[3], 1)]
    gate_up_ring.step()
    out_send = call(
        "out_send", add_body, [block_low], [parts[2], out_got[1]], deps=out_got[:1]
    )
    out_far = swap(out_send, 2)
    dq_far, dkv = call(
        "attention_back_far",
        back_far_body,
        [heads_low, ((KV_COLS, length), BF)],
        [
            *(mixed[2], mixed[3], out_full, q, k, k_rows, v_rows, o_far, lse_far, cosine, sine),
            *(dk, dv),
        ],
        [place, prefix],
        scratch=[pltpu.VMEM((PAIR, length, HD), F32)] * 2 + held,
    )
    gate_up_ring.step(down_ring.got)
    one_keep, one_far_keep, one_sends, last = last_grad(
        rows_one,
        mixed,
        token_blocks,
        inv_rows,
        first_full,
        dkv,
        (dq_near, dq_far),
        (o_near, o_far),
        gain_two,
        (),
    )
    last_ring = Scatter(last, place, gate_up_ring.got)
    gate_up_sum, gate_up_squares = ring_kernel(
        "gate_up_sum",
        sum_body,
        [((share, 2 * hidden), F32), ((1,), F32)],
        place,
        gate_up_ring.terms[0],
        (0,),
        gate_up_ring.terms[1:],
    )
    down_sum, down_squares = ring_kernel(
        "down_sum",
        sum_body,
        [((share, hidden), F32), ((1,), F32)],
        place,
        down_ring.terms[0],
        (0,),
        down_ring.terms[1:],
    )
    last_ring.step()
    one_got = swap(relay(one_sends)[0], 1)
    one_send = call("one_send", add_second_body, [block_low], [one_far_keep, one_got])
    one_far = swap(one_send, 2)
    held_weights = hold(
        (
            *(query_weight, query_first, query_second),
            *(keyval_weight, keyval_first, keyval_second),
            *(outproj_weight.T, outproj_first.T, outproj_second.T),
            gate_up_weight,
        ),
    )
    last_ring.step()
    held_weights += hold(
        (gate_up_first, gate_up_second, down_weight.T, down_first.T, down_second.T)
    )
    last_ring.step()
    output = call(
        "output", output_body, [block_low], [parts[0], out_got[0], out_far, mixed_one], far=(0,)
    )
    last_sum, shared = ring_kernel(
        "pack",
        pack_body,
        [((share, first_columns), F32), ((share, KV_COLS + GAIN_COLS), BF)],
        place,
        last_ring.terms[0],
        (0,),
        last_ring.terms[1:],
        [gate_up_squares, down_squares],
    )
    shared_blocks = gather_blocks(shared)
    input_grad = call(
        "input_grad",
        input_grad_body,
        [block_float],
        [one_keep, one_got, one_far, tokens, mixed_grad, gains],
        far=(0,),
    )
    keyval_total, gains_total, squares = call(
        "shared_sums",
        shared_body,
        [((share, 2 * KV * HD), F32), ((8, share), F32), ((8, 128), F32)],
        shared_blocks,
        [place],
        scratch=[pltpu.VMEM((TENSOR, share, KV_COLS + GAIN_COLS), F32)],
    )
    square_total = sum_over_dp(squares)
    params_all = D * HEADS * HD + 2 * D * KV * HD + HEADS * HD * D + 2 * D * FF + FF * D + 2 * D
    limit = 0.01 * math.sqrt(replica_count * length * params_all)
    updates = adam_all(
        limit,
        square_total,
        gains_total,
        (norm_gains, gains_first, gains_second),
        (keyval_total, last_sum, gate_up_sum, down_sum),
        held_weights,
    )
    return (
        output[None],
        input_grad[None],
        *updates[:6],
        *(update.T for update in updates[6:9]),
        *updates[9:12],
        *(update.T for update in updates[12:15]),
        *updates[15:18],
        updates[18][0],
    )


def solution(mesh):
    rows = P("dp", "tensor", None)
    weights = (
        (P("dp", "tensor"),) * 3
        + (P("dp", None),) * 3
        + (P("tensor", "dp"),) * 3
        + (P(None, "dp", "tensor"),) * 3
        + (P("tensor", "dp"),) * 3
        + (P(None, "dp"),) * 3
    )
    return jax.shard_map(
        per_device,
        mesh=mesh,
        in_specs=(rows, P("dp"), rows) + weights,
        out_specs=(rows, rows) + weights + (P(),),
        check_vma=False,
    )
```

```python
import functools
import math

import jax
import jax.numpy as jnp
import numpy as np
from jax import lax
from jax.experimental import pallas as pl
from jax.experimental.pallas import tpu as pltpu
from jax.sharding import PartitionSpec as P

D = 1280
HEADS = 20
KV = 5
HD = 64
FF = 3584
STEP = 5


EPSILON = 1e-05
BETA_ONE = 0.5
BETA_TWO = 0.6
ADAM_EPSILON = 1e-08
DECAY_RATE = 0.1
MASKED = -1e30

TENSOR = 4
GROUP = HEADS // TENSOR
SHARE = HEADS // KV
PAIR = 2
BLOCK = 256
PREFIX_MAX = 512
KV_COLS = 2 * PAIR * HD
Q_COLS = GROUP * HD
GAIN_COLS = 64
BF = jnp.bfloat16
F32 = jnp.float32


def rope_tables(length):
    position = np.arange(length, dtype=np.float32)
    frequency = (10000.0 ** (-(2.0 / HD) * np.arange(HD // 2))).astype(np.float32)
    angles = (frequency[:, None] * position[None, :]).astype(np.float32).astype(np.float64)
    return np.cos(angles).astype(np.float32), np.sin(angles).astype(np.float32)


def dot(left, right, left_dim, right_dim):
    return lax.dot_general(
        left, right, (((left_dim,), (right_dim,)), ((), ())), preferred_element_type=F32
    )


def norm_back(grad_normed, values_hat, inv_root, gain):
    scaled = grad_normed * gain
    return inv_root * (scaled - values_hat * jnp.mean(values_hat * scaled, axis=-1, keepdims=True))


def inverse_root(values):
    return lax.rsqrt(jnp.mean(values * values, axis=-1, keepdims=True) + EPSILON)


def adam_step(weight, first, second, gradient, rate, clip):
    clipped = gradient * clip
    first_new = BETA_ONE * first + (1.0 - BETA_ONE) * clipped
    second_new = BETA_TWO * second + (1.0 - BETA_TWO) * clipped * clipped
    corrected_one = first_new / (1.0 - BETA_ONE**STEP)
    corrected_two = second_new / (1.0 - BETA_TWO**STEP)
    weight_new = weight - rate * (
        corrected_one / (jnp.sqrt(corrected_two) + ADAM_EPSILON) + DECAY_RATE * weight
    )
    return (first_new, second_new, weight_new)


def swap(values, distance):
    return lax.ppermute(values, "tensor", [(i, i ^ distance) for i in range(TENSOR)])


def gather_blocks(rows):
    far = swap(rows, 2)
    near = swap(rows, 1)
    return [rows, near, far, swap(far, 1)]


def ring_order(count):
    return list(range(0, count, 2)) + list(range(count - 1, 0, -2))


OFFSETS = (0, -1, 1, -2, 2, -3, 3, 4)


def place_table(count):
    order = ring_order(count)
    table = np.zeros((count * TENSOR, 16), np.int32)
    for position, owner in enumerate(order):
        for group in range(TENSOR):
            row = table[owner * TENSOR + group]
            row[0] = group
            row[1 : 1 + len(OFFSETS)] = [order[(position + o) % count] for o in OFFSETS]
    return table


def ring_pass(values, step):
    order = ring_order(lax.axis_size("dp"))
    count = len(order)
    return lax.ppermute(
        values, "dp", [(order[q], order[(q + step) % count]) for q in range(count)]
    )


TRAIL = [None]
LIGHT = pl.CostEstimate(flops=1024, bytes_accessed=1024, transcendentals=0)


def in_order(name, deps, operands, build):
    deps = list(deps)
    last = TRAIL[0]
    if last is not None and all(last is not operand for operand in (*operands, *deps)):
        deps.append(last)
    result = build(deps)
    arrays = [array for array in result if array.size > 1]
    TRAIL[0] = arrays[0]
    return result


def call(
    name, body, outs, ins=(), scalars=(), deps=(), scratch=(), mib=28, far=()
):
    def kernel(*refs):
        lead = len(scalars) + len(ins)
        sources, rest = refs[:lead], refs[lead + dep_count :]
        targets, rest = list(rest[: len(outs)]), rest[len(outs) :]
        stages, rest = rest[: len(far)], rest[len(far) :]
        copies = []
        for place, (index, stage) in enumerate(zip(far, stages)):
            copies.append(pltpu.make_async_copy(stage, targets[index], rest[-1].at[place]))
            targets[index] = stage
        body(*sources, *targets, *(rest[:-1] if far else rest))
        for copy in copies:
            copy.start()
        for copy in copies:
            copy.wait()

    def spec(shape):
        rank = len(shape)
        return pl.BlockSpec(shape, lambda i: (0,) * rank, pipeline_mode=pl.Buffered(1))

    def out_spec(index, shape):
        if index in far:
            return pl.BlockSpec(memory_space=pltpu.HBM)
        if shape == (1,):
            return pl.BlockSpec(memory_space=pltpu.SMEM)
        return spec(shape)

    scratch = [pltpu.VMEM(*outs[index]) for index in far] + list(scratch)
    if far:
        scratch.append(pltpu.SemaphoreType.DMA((len(far),)))
    dep_count = 0

    def build(deps):
        nonlocal dep_count
        dep_count = len(deps)
        return pl.pallas_call(
            kernel,
            grid=(1,),
            out_shape=tuple(jax.ShapeDtypeStruct(shape, kind) for shape, kind in outs),
            in_specs=[pl.BlockSpec(memory_space=pltpu.SMEM)] * len(scalars)
            + [spec(a.shape) for a in ins]
            + [pl.BlockSpec(memory_space=pl.ANY)] * len(deps),
            out_specs=tuple(out_spec(index, shape) for index, (shape, _) in enumerate(outs)),
            scratch_shapes=scratch,
            compiler_params=pltpu.CompilerParams(vmem_limit_bytes=mib << 20),
            cost_estimate=LIGHT,
            name=name,
        )(*scalars, *ins, *deps)

    result = in_order(name, deps, ins, build)
    return result[0] if len(outs) == 1 else result


def ring_send(ahead, behind):
    return ring_pass(ahead, 1), ring_pass(behind, -1)


def copy_body(*refs):
    count = len(refs) // 2
    for source, target in zip(refs[:count], refs[count:]):
        target[...] = source[...]


def relay(*arrays, deps=()):
    result = call("relay", copy_body, [(a.shape, a.dtype) for a in arrays], arrays, deps=deps)
    return result if len(arrays) > 1 else [result]


class Gather:
    def __init__(self, shard):
        self.pieces = [shard]
        self.ring = lax.axis_size("dp") == 8
        if self.ring:
            self.send(shard, shard)
        else:
            self.pieces = [lax.all_gather(shard, "dp", axis=0, tiled=True)]

    def send(self, ahead, behind):
        self.got = ring_send(ahead, behind)
        self.pieces += self.got

    def forward(self):
        if self.ring:
            self.send(*self.got)

    def relay(self, deps=()):
        if self.ring:
            self.send(*relay(*self.got, deps=deps))

    def halve(self):
        if not self.ring:
            return
        rows, columns = self.pieces[0].shape
        half = rows // 2

        def body(ahead, behind, upper, lower):
            upper[...] = ahead[pl.ds(0, half), :]
            lower[...] = behind[pl.ds(half, half), :]

        self.send(*call("halve", body, [((half, columns), BF)] * 2, self.got))

    def place(self, place, width):
        if not self.ring:
            return self.pieces[0]

        def body(place, *refs):
            put_pieces(place, refs[:-1], refs[-1])

        shape = (width, self.pieces[0].shape[1])
        return call("place_shards", body, [(shape, BF)], self.pieces, [place])


def put_pieces(place, pieces, full):
    if len(pieces) == 1:
        full[...] = pieces[0][...]
        return
    rows = pieces[0].shape[0]
    half = rows // 2
    whole_pieces = len(pieces) - 2
    for index, piece in enumerate(pieces):
        owner = place[1 + min(index, whole_pieces)]
        start = owner * rows + max(index - whole_pieces, 0) * half
        full[pl.ds(pl.multiple_of(start, half), piece.shape[0]), :] = piece[...]


def ring_kernel(name, body, outs, place, partial, picks, ins=(), scalars=(), deps=()):
    rows, columns = outs[0][0][0], partial.shape[1]
    if not picks or partial.shape[0] == rows:
        picks, block_rows = picks or (0,), partial.shape[0]
        blocks = [pl.BlockSpec((block_rows, columns), lambda i, s: (0, 0))] * len(picks)
    else:
        block_rows = partial.shape[0] // lax.axis_size("dp")
        blocks = [
            pl.BlockSpec((block_rows, columns), functools.partial(pick_block, 1 + OFFSETS.index(o)))
            for o in picks
        ]

    def kernel(_, *refs):
        lead = len(scalars) + len(picks) + len(ins)
        body(*refs[:lead], *refs[lead + dep_count :])

    dep_count = 0

    def fixed(shape):
        if shape == (1,):
            return pl.BlockSpec(memory_space=pltpu.SMEM)
        return pl.BlockSpec(shape, lambda i, s: (0, 0))

    def build(deps):
        nonlocal dep_count
        dep_count = len(deps)
        return pl.pallas_call(
            kernel,
            grid_spec=pltpu.PrefetchScalarGridSpec(
                num_scalar_prefetch=1,
                grid=(1,),
                in_specs=[pl.BlockSpec(memory_space=pltpu.SMEM)] * len(scalars)
                + blocks
                + [fixed(a.shape) for a in ins]
                + [pl.BlockSpec(memory_space=pl.ANY)] * len(deps),
                out_specs=tuple(fixed(shape) for shape, _ in outs),
            ),
            out_shape=tuple(jax.ShapeDtypeStruct(shape, kind) for shape, kind in outs),
            compiler_params=pltpu.CompilerParams(vmem_limit_bytes=24 << 20),
            cost_estimate=LIGHT,
            name=name,
        )(place, *scalars, *[partial] * len(picks), *ins, *deps)

    return in_order(name, deps, (partial, *ins), build)


def pick_block(column, i, place):
    return (place[column], 0)


def far_body(block, upper, lower):
    half = upper.shape[0]
    upper[...] = block[pl.ds(0, half), :]
    lower[...] = block[pl.ds(half, half), :]


def half_step_body(more, less, ahead, behind, more_out, less_out):
    half = ahead.shape[0]
    upper, lower = pl.ds(0, half), pl.ds(half, half)
    more_out[upper, :] = (more[upper, :].astype(F32) + ahead[...].astype(F32)).astype(BF)
    more_out[lower, :] = more[lower, :]
    less_out[upper, :] = less[upper, :]
    less_out[lower, :] = (less[lower, :].astype(F32) + behind[...].astype(F32)).astype(BF)


def step_body(more, less, ahead, behind, more_out, less_out):
    more_out[...] = (more[...].astype(F32) + ahead[...].astype(F32)).astype(BF)
    less_out[...] = (less[...].astype(F32) + behind[...].astype(F32)).astype(BF)


class Scatter:
    def __init__(self, partial, place, deps=()):
        self.count = lax.axis_size("dp")
        self.partial, self.place = partial, place
        self.offset = 4
        if self.count != 8:
            total = lax.psum_scatter(partial, "dp", scatter_dimension=0, tiled=True)
            self.terms = [total, jnp.zeros_like(total), jnp.zeros_like(total)]
            self.got = ()
            return
        self.rows, self.columns = partial.shape[0] // self.count, partial.shape[1]
        self.run("scatter_first", far_body, self.rows // 2, (4,), (), deps)

    def run(self, name, body, rows, picks, arrived, deps=()):
        outs = [((rows, self.columns), BF)] * 2
        sends = ring_kernel(
            name, body, outs, self.place, self.partial, picks, arrived, deps=deps
        )
        self.got = ring_send(*sends)
        self.offset -= 1
        self.terms = [self.partial, *self.got]

    def step(self, deps=()):
        if self.count == 8:
            body = half_step_body if self.offset == 3 else step_body
            picks = (self.offset, -self.offset)
            self.run("scatter_step", body, self.rows, picks, self.got, deps)


def sum_body_two(left, right, out):
    out[...] = left[...] + right[...]


def sum_over_dp(value):
    distance = 1
    while distance < lax.axis_size("dp"):
        pairs = [(i, i ^ distance) for i in range(lax.axis_size("dp"))]
        other = lax.ppermute(value, "dp", pairs)
        value = call("norm_sum", sum_body_two, [(value.shape, F32)], [value, other])
        distance *= 2
    return value


def turn(upper, lower, cosine, sine):
    return upper * cosine - lower * sine, lower * cosine + upper * sine


def key_blocks(block):
    return max(block + 1, PREFIX_MAX // BLOCK)


def visible_keys(block, other, prefix):
    if other < block:
        return None
    keys = other * BLOCK + lax.broadcasted_iota(jnp.int32, (BLOCK, BLOCK), 0)
    queries = block * BLOCK + lax.broadcasted_iota(jnp.int32, (BLOCK, BLOCK), 1)
    return (keys <= queries) | (keys < prefix)


def lanes(index, size=BLOCK):
    return pl.ds(pl.multiple_of(index * size, size), size)


def query_blocks(group, side, work):
    for chip in range(TENSOR // 2):

        @pl.when(((group >> 1) ^ side) == chip)
        def _():
            for block in (2 * chip, 2 * chip + 1):
                work(block, (block ^ group) & 1)


def attend(group, prefix, side, q, k_rows, v, o_out, lse_out):
    def work(block, slot):
        here, target = pl.ds(block * BLOCK, BLOCK), lanes(slot)

        @pl.loop(0, GROUP)
        def _(head):
            own = jnp.where(head + group >= SHARE, 1, 0)
            query = q[lanes(head, HD), here]
            scores = []
            for other in range(key_blocks(block)):
                raw = dot(k_rows[own, pl.ds(other * BLOCK, BLOCK), :], query, 1, 0)
                mask = visible_keys(block, other, prefix)
                scores.append(raw if mask is None else jnp.where(mask, raw, MASKED))
            highest = jnp.max(functools.reduce(jnp.maximum, scores), axis=0, keepdims=True)
            total = jnp.zeros((1, BLOCK), F32)
            attended = jnp.zeros((HD, BLOCK), F32)
            for other, score in enumerate(scores):
                weight = jnp.exp(score - highest)
                total += jnp.sum(weight, axis=0, keepdims=True)
                attended += dot(
                    v[lanes(own, HD), pl.ds(other * BLOCK, BLOCK)], weight.astype(BF), 1, 0
                )
            o_out[lanes(head, HD), target] = (attended / total).astype(BF)
            lse_out[pl.ds(head, 1), target] = highest + jnp.log(total)

    query_blocks(group, side, work)


def project_out(o, weight, outs):
    for slot, out in enumerate(outs):
        out[...] = dot(o[:, pl.ds(slot * BLOCK, BLOCK)], weight[...], 0, 1).astype(BF)


def front_body(count, place, prefix, *refs):
    pieces, refs = refs[:count], refs[count:]
    tokens, refs = refs[:TENSOR], refs[TENSOR:]
    cosine, sine, full, out_w, gains, rows_one, inv_rows, q, k, v, k_rows, v_rows = refs[:12]
    o_out, lse_out, keep, send = refs[12:]
    group = place[0]
    half = HD // 2
    put_pieces(place, pieces, full)
    out_w[...] = full[:, pl.ds(KV_COLS + Q_COLS + GAIN_COLS, Q_COLS)]
    qkv_w = full[:, pl.ds(0, KV_COLS + Q_COLS)]
    gain_rows = full[:, pl.ds(KV_COLS + Q_COLS, GAIN_COLS)].astype(F32).T[:8]
    gains[...] = gain_rows
    for index in range(TENSOR):
        rows = pl.ds(index * BLOCK, BLOCK)
        values = tokens[index][...].astype(F32)
        inv = inverse_root(values)
        inv_rows[rows, :] = inv
        normed = (values * inv * gain_rows[:1]).astype(BF)
        rows_one[rows, :] = normed
        flat = dot(normed, qkv_w, 1, 0)
        block = index ^ group
        here = lanes(block)
        cos, sin = cosine[:, here], sine[:, here]
        turned = flat.T
        for head in range(PAIR + GROUP):
            row = head * HD if head < PAIR else KV_COLS + (head - PAIR) * HD
            upper, lower = turn(turned[row : row + half], turned[row + half : row + HD], cos, sin)
            both = jnp.concatenate([upper, lower], axis=0)
            if head < PAIR:
                k[pl.ds(row, HD), here] = both.astype(BF)
                k_rows[head, here, :] = both.T.astype(BF)
            else:
                scaled = both.astype(BF) * jnp.asarray(HD**-0.5, BF)
                q[pl.ds(row - KV_COLS, HD), here] = scaled
        v[:, here] = turned[PAIR * HD : KV_COLS].astype(BF)
        for head in range(PAIR):
            start = (PAIR + head) * HD
            v_rows[head, here, :] = flat[:, start : start + HD].astype(BF)
    attend(group, prefix[0], 1, q, k_rows, v, o_out, lse_out)
    project_out(o_out, out_w, (keep, send))


def near_body(place, prefix, q, k_rows, v, out_w, o_out, lse_out, keep, send):
    attend(place[0], prefix[0], 0, q, k_rows, v, o_out, lse_out)
    project_out(o_out, out_w, (keep, send))


def attend_back(side, place, prefix, mixed, out_w, q, k, k_rows, v_rows, o, lse, cosine, sine, dq, dk, dv, grad):
    group, prefix = place[0], prefix[0]
    half = HD // 2
    for slot in range(2):
        grad[:, pl.ds(slot * BLOCK, BLOCK)] = dot(mixed[slot][...], out_w[...], 1, 0).T.astype(BF)

    def work(block, slot):
        here, target = pl.ds(block * BLOCK, BLOCK), lanes(slot)

        @pl.loop(0, GROUP)
        def _(head):
            own = jnp.where(head + group >= SHARE, 1, 0)
            rows = lanes(head, HD)
            query = q[rows, here]
            grad_here = grad[rows, target]
            inner = jnp.sum(
                grad_here.astype(F32) * o[rows, target].astype(F32), axis=0, keepdims=True
            )
            logs = lse[pl.ds(head, 1), target]
            total = jnp.zeros((HD, BLOCK), F32)
            for other in range(key_blocks(block)):
                there = pl.ds(other * BLOCK, BLOCK)
                probs = jnp.exp(dot(k_rows[own, there, :], query, 1, 0) - logs)
                mask = visible_keys(block, other, prefix)
                if mask is not None:
                    probs = jnp.where(mask, probs, 0.0)
                prob_grad = dot(v_rows[own, there, :], grad_here, 1, 0)
                score_grad = (probs * (prob_grad - inner)).astype(BF)
                total += dot(k[lanes(own, HD), there], score_grad, 1, 0)
                dk[own, there, :] += dot(score_grad, query, 1, 1)
                dv[own, there, :] += dot(probs.astype(BF), grad_here, 1, 1)
            total = total * HD**-0.5
            upper, lower = turn(total[:half], total[half:], cosine[:, here], -sine[:, here])
            dq[rows, target] = jnp.concatenate([upper, lower], axis=0).astype(BF)

    query_blocks(group, side, work)


def back_near_body(place, prefix, m0, m1, out_w, q, k, k_rows, v_rows, o, lse, cosine, sine, dq, dk, dv, grad):
    dk[...] = jnp.zeros_like(dk)
    dv[...] = jnp.zeros_like(dv)
    attend_back(
        0, place, prefix, (m0, m1), out_w, q, k, k_rows, v_rows, o, lse, cosine, sine, dq, dk, dv, grad
    )


def back_far_body(
    place, prefix, m0, m1, out_w, q, k, k_rows, v_rows, o, lse, cosine, sine, dk_in, dv_in, dq, dkv, dk, dv, grad
):
    half = HD // 2
    dk[...] = dk_in[...]
    dv[...] = dv_in[...]
    attend_back(
        1, place, prefix, (m0, m1), out_w, q, k, k_rows, v_rows, o, lse, cosine, sine, dq, dk, dv, grad
    )
    for block in range(TENSOR):
        here, target = pl.ds(block * BLOCK, BLOCK), lanes(block ^ place[0])
        for head in range(PAIR):
            turned = dk[head, here, :].T
            upper, lower = turn(turned[:half], turned[half:], cosine[:, here], -sine[:, here])
            dkv[pl.ds(head * HD, HD), target] = jnp.concatenate([upper, lower], axis=0).astype(BF)
            dkv[pl.ds((PAIR + head) * HD, HD), target] = dv[head, here, :].T.astype(BF)


def norm_body(tokens, keep, near, far, gains, mixed, normed):
    values = tokens[...].astype(F32) + (
        (keep[...].astype(F32) + near[...].astype(F32)) + far[...].astype(F32)
    )
    mixed[...] = values
    normed[...] = (values * inverse_root(values) * gains[1:2]).astype(BF)


def norm_back_body(keep, near, far, mixed, cotangent, gains, grad, grad_low, gain_grad):
    normed_grad = (keep[...].astype(F32) + near[...].astype(F32)) + far[...].astype(F32)
    values = mixed[...]
    inv = inverse_root(values)
    hat = values * inv
    gain_grad[...] = jnp.broadcast_to(
        jnp.sum(normed_grad * hat, axis=0, keepdims=True), gain_grad.shape
    )
    total = cotangent[...].astype(F32) + norm_back(normed_grad, hat, inv, gains[1:2])
    grad[...] = total
    grad_low[...] = total.astype(BF)


def input_grad_body(keep, nears, far, tokens, mixed_grad, gains, out):
    near = nears[pl.ds(0, BLOCK), :].astype(F32)
    normed_grad = (keep[...].astype(F32) + near) + far[...].astype(F32)
    values = tokens[...].astype(F32)
    inv = inverse_root(values)
    out[...] = mixed_grad[...] + norm_back(normed_grad, values * inv, inv, gains[0:1])


def output_body(keep, near, far, mixed, out):
    out[...] = (
        mixed[...] + ((keep[...].astype(F32) + near[...].astype(F32)) + far[...].astype(F32))
    ).astype(BF)


def add_second_body(left, rights, out):
    right = rights[pl.ds(BLOCK, BLOCK), :]
    out[...] = (left[...].astype(F32) + right.astype(F32)).astype(BF)


def add_body(left, right, out):
    out[...] = (left[...].astype(F32) + right[...].astype(F32)).astype(BF)


def hidden_body(a0, a1, weight, by_gate, by_up, hidden):
    columns = hidden.shape[1]
    for slot, rows in enumerate((a0, a1)):
        both = dot(rows[...], weight[:, pl.ds(0, 2 * columns)], 1, 0)
        gate, up = both[:, :columns], both[:, columns:]
        sigma = jax.nn.sigmoid(gate)
        silu = gate * sigma
        here = pl.ds(slot * BLOCK, BLOCK)
        by_gate[here, :] = (up * sigma * (1.0 + gate * (1.0 - sigma))).astype(BF)
        by_up[here, :] = silu.astype(BF)
        hidden[here, :] = (silu * up).astype(BF)


def hidden_back_body(c0, c1, weight, by_gate, by_up, grads, part0, part1):
    columns = by_gate.shape[1]
    for slot, (rows, part) in enumerate(((c0, part0), (c1, part1))):
        here = pl.ds(slot * BLOCK, BLOCK)
        grad = dot(rows[...], weight[:, pl.ds(2 * columns, columns)], 1, 0)
        grads[here, pl.ds(0, columns)] = (grad * by_gate[here, :].astype(F32)).astype(BF)
        grads[here, pl.ds(columns, columns)] = (grad * by_up[here, :].astype(F32)).astype(BF)
        part[...] = dot(grads[here, :], weight[:, pl.ds(0, 2 * columns)], 1, 1).astype(BF)


def down_body(near, far, weight, *parts):
    columns = near.shape[1]
    down = weight[:, pl.ds(2 * columns, columns)]
    for index, part in enumerate(parts):
        source = (near, far)[index // 2]
        part[...] = dot(source[pl.ds(index % 2 * BLOCK, BLOCK), :], down, 1, 1).astype(BF)


def column_grad(lefts, rights):
    width, columns = lefts[0].shape[1], rights[0].shape[1]
    tile = 256

    def kernel(*refs):
        left = jnp.concatenate([ref[...] for ref in refs[:TENSOR]], axis=0)
        right = jnp.concatenate([ref[...] for ref in refs[TENSOR : TENSOR + 2]], axis=0)
        refs[-1][...] = dot(left, right, 0, 0).astype(BF)

    length = TENSOR * BLOCK

    def build(deps):
        return pl.pallas_call(
            kernel,
            grid=(width // tile,),
            out_shape=(jax.ShapeDtypeStruct((width, columns), BF),),
            in_specs=[pl.BlockSpec((BLOCK, tile), lambda i: (0, i))] * TENSOR
            + [pl.BlockSpec(right.shape, lambda i: (0, 0)) for right in rights]
            + [pl.BlockSpec(memory_space=pl.ANY)] * len(deps),
            out_specs=(pl.BlockSpec((tile, columns), lambda i: (i, 0)),),
            compiler_params=pltpu.CompilerParams(vmem_limit_bytes=28 << 20),
            cost_estimate=LIGHT,
            name="column_grad",
        )(*lefts, *rights, *deps)

    return in_order("column_grad", (), (*lefts, *rights), build)[0]


def last_grad_kernel(rows_one, *refs):
    mixed, refs = refs[:TENSOR], refs[TENSOR:]
    tokens, refs = refs[:TENSOR], refs[TENSOR:]
    inv_rows, weight, dkv, dq_near, dq_far, o_near, o_far, gain_two = refs[:8]
    keep, far_keep, sends, out = refs[-4:]
    tile = rows_one.shape[1]
    grads = jnp.concatenate(
        [dkv[...], jnp.concatenate([dq_near[...], dq_far[...]], axis=1)], axis=0
    )
    spread = dot(weight[:, pl.ds(0, KV_COLS + Q_COLS)], grads, 1, 0).T
    gain_one = jnp.zeros((1, tile), F32)
    for index in range(TENSOR):
        here = slice(index * BLOCK, (index + 1) * BLOCK)
        block = spread[here]
        if index % 2:
            sends[pl.ds(index // 2 * BLOCK, BLOCK), :] = block.astype(BF)
        else:
            (keep, far_keep)[index // 2][...] = block.astype(BF)
        hat = tokens[index][...].astype(F32) * inv_rows[here, :]
        gain_one += jnp.sum(block * hat, axis=0, keepdims=True)
    rows = jnp.concatenate(
        [
            dot(grads, rows_one[...], 1, 0),
            gain_one,
            gain_two[0:1],
            jnp.zeros((GAIN_COLS - 2, tile), F32),
        ],
        axis=0,
    )
    columns = rows.shape[0]
    out[:, pl.ds(0, columns)] = rows.T.astype(BF)
    attended = jnp.concatenate([o_near[...], o_far[...]], axis=1)
    mixed_all = jnp.concatenate([block[...] for block in mixed], axis=0)
    out[:, pl.ds(columns, Q_COLS)] = dot(attended, mixed_all, 1, 0).T.astype(BF)


def last_grad(rows_one, mixed, tokens, inv_rows, weight, dkv, dq, o, gain_two, deps):
    length, width = rows_one.shape
    columns = KV_COLS + Q_COLS + GAIN_COLS + Q_COLS
    tile = 256
    by_block = pl.BlockSpec((BLOCK, tile), lambda i: (0, i))

    def fixed(array):
        return pl.BlockSpec(array.shape, lambda i: (0, 0))

    operands = (rows_one, *mixed, *tokens, inv_rows, weight, dkv, *dq, *o, gain_two)

    def build(deps):
        return pl.pallas_call(
            last_grad_kernel,
            grid=(width // tile,),
            out_shape=tuple(
                jax.ShapeDtypeStruct((c, width), BF) for c in (BLOCK, BLOCK, 2 * BLOCK)
            )
            + (jax.ShapeDtypeStruct((width, columns), BF),),
            in_specs=[pl.BlockSpec((length, tile), lambda i: (0, i))]
            + [by_block] * (2 * TENSOR)
            + [
                fixed(inv_rows),
                pl.BlockSpec((tile, weight.shape[1]), lambda i: (i, 0)),
                fixed(dkv),
                *(fixed(array) for array in (*dq, *o)),
                pl.BlockSpec((8, tile), lambda i: (0, i)),
            ]
            + [pl.BlockSpec(memory_space=pl.ANY)] * len(deps),
            out_specs=(by_block, by_block, pl.BlockSpec((2 * BLOCK, tile), lambda i: (0, i)))
            + (pl.BlockSpec((tile, columns), lambda i: (i, 0)),),
            compiler_params=pltpu.CompilerParams(vmem_limit_bytes=32 << 20),
            cost_estimate=LIGHT,
            name="last_grad",
        )(*operands, *deps)

    return in_order("last_grad", deps, operands, build)


def cast_first_body(place, keyval, query, outproj, gains, out):
    for index in range(2):
        start = index * KV * HD
        chosen = keyval[:, pl.ds(start, PAIR * HD)]
        for group in range(1, TENSOR):
            chosen = jnp.where(
                place[0] == group, keyval[:, pl.ds(start + group * HD, PAIR * HD)], chosen
            )
        out[:, pl.ds(index * PAIR * HD, PAIR * HD)] = chosen.astype(BF)
    rows = gains.shape[1]
    filled = jnp.concatenate([gains[...], jnp.zeros((GAIN_COLS - 2, rows), F32)], axis=0)
    out[:, pl.ds(KV_COLS, Q_COLS + GAIN_COLS)] = jnp.concatenate(
        [query[...], filled.T], axis=1
    ).astype(BF)
    out[:, pl.ds(KV_COLS + Q_COLS + GAIN_COLS, Q_COLS)] = outproj[...].astype(BF)


def cast_mlp_body(gate_up, down, out):
    columns = down.shape[1]
    for index, source in enumerate((gate_up[0], gate_up[1], down[...])):
        out[:, pl.ds(index * columns, columns)] = source.astype(BF)


def cast_body(weight, out):
    out[...] = weight[...].astype(BF)


def sum_body(block, ahead, behind, total, squares):
    values = block[...].astype(F32) + (ahead[...].astype(F32) + behind[...].astype(F32))
    total[...] = values
    squares[0] = jnp.sum(values * values)


def pack_body(gate_up_squares, down_squares, block, ahead, behind, total, shared):
    values = block[...].astype(F32) + (ahead[...].astype(F32) + behind[...].astype(F32))
    total[...] = values
    query = values[:, KV_COLS : KV_COLS + Q_COLS]
    outproj = values[:, KV_COLS + Q_COLS + GAIN_COLS :]
    own = jnp.sum(query * query, axis=0, keepdims=True)
    own = jnp.sum(own + jnp.sum(outproj * outproj, axis=0, keepdims=True), axis=1, keepdims=True)
    own = own + (gate_up_squares[0] + down_squares[0])
    first = own.astype(BF).astype(F32)
    second = (own - first).astype(BF).astype(F32)
    third = (own - first - second).astype(BF).astype(F32)
    gains = values[:, KV_COLS + Q_COLS : KV_COLS + Q_COLS + GAIN_COLS]
    lane = lax.broadcasted_iota(jnp.int32, gains.shape, 1)
    for index, part in enumerate((first, second, third)):
        gains = jnp.where(lane == 2 + index, part, gains)
    shared[...] = jnp.concatenate([values[:, :KV_COLS], gains], axis=1).astype(BF)


def shared_body(place, own, near, far, far_near, keyval, gains, squares, by_index):
    for index, piece in enumerate((own, near, far, far_near)):
        by_index[index ^ place[0]] = piece[...].astype(F32)
    gains_sum = functools.reduce(
        jnp.add, [by_index[index, :, pl.ds(KV_COLS, GAIN_COLS)] for index in range(TENSOR)]
    )
    rows = gains_sum.T[:8]
    gains[...] = rows
    heads = []
    for start in (0, PAIR * HD):
        for head in range(KV):
            readers = []
            if head < TENSOR:
                readers.append(by_index[head, :, pl.ds(start, HD)])
            if head > 0:
                readers.append(by_index[head - 1, :, pl.ds(start + HD, HD)])
            heads.append(sum(readers[1:], readers[0]))
    total = jnp.concatenate(heads, axis=1)
    keyval[...] = total
    squares[...] = jnp.full(
        squares.shape,
        jnp.sum(total * total) + jnp.sum(rows[:2] * rows[:2]) + jnp.sum(rows[2:5, :1]),
    )


def hold_body(*refs):
    count = (len(refs) - 1) // 2
    copies = [
        pltpu.make_async_copy(refs[index], refs[count + index], refs[-1].at[index])
        for index in range(count)
    ]
    for copy in copies:
        copy.start()
    for copy in copies:
        copy.wait()


def hold(arrays):
    dep_count = 0

    def kernel(*refs):
        hold_body(*refs[: len(arrays)], *refs[len(arrays) + dep_count :])

    def build(deps):
        nonlocal dep_count
        dep_count = len(deps)
        return pl.pallas_call(
            kernel,
            out_shape=tuple(jax.ShapeDtypeStruct(array.shape, array.dtype) for array in arrays),
            in_specs=[pl.BlockSpec(memory_space=pltpu.HBM)] * len(arrays)
            + [pl.BlockSpec(memory_space=pl.ANY)] * len(deps),
            out_specs=tuple([pl.BlockSpec(memory_space=pltpu.VMEM)] * len(arrays)),
            scratch_shapes=[pltpu.SemaphoreType.DMA((len(arrays),))],
            compiler_params=pltpu.CompilerParams(vmem_limit_bytes=52 << 20),
            cost_estimate=LIGHT,
            name="hold",
        )(*arrays, *deps)

    return in_order("hold", (), arrays, build)


def adam_kernel(limit, total, gains_grad, gains, gains_first, gains_second, *refs):
    count = 5
    keyval_grad, last_grad, gate_up_grad, down_grad = refs[:4]
    weights, outs = refs[4 : 4 + 3 * count], refs[4 + 3 * count :]
    norm = jnp.sqrt(total[...])
    clip = limit / jnp.maximum(norm[0:1, 0:1], limit)
    outs[-1][0] = jnp.max(norm)
    gains_out = outs[3 * count : 3 * count + 3]
    gains_out[0][...], gains_out[1][...], gains_out[2][...] = adam_step(
        gains[...], gains_first[...], gains_second[...], gains_grad[0:2], 0.25, clip
    )
    tile = keyval_grad.shape[0]
    here = pl.ds(0, tile)
    if weights[0].shape[0] > tile:
        here = pl.ds(pl.multiple_of(pl.program_id(0) * tile, tile), tile)
    hidden = down_grad.shape[1]
    out_start = KV_COLS + Q_COLS + GAIN_COLS
    grads = (
        last_grad[:, pl.ds(KV_COLS, Q_COLS)],
        keyval_grad[...],
        last_grad[:, pl.ds(out_start, Q_COLS)],
        None,
        down_grad[...],
    )
    rates = (
        0.5 / math.sqrt(D),
        0.5 / math.sqrt(D),
        2.0 / math.sqrt(HEADS * HD),
        0.5 / math.sqrt(D),
        0.5 / math.sqrt(FF),
    )
    for index in range(count):
        held = weights[3 * index : 3 * index + 3]
        first_new, second_new, weight_new = outs[3 * index : 3 * index + 3]
        if grads[index] is None:
            for side in range(2):
                first_new[side], second_new[side], weight_new[side] = adam_step(
                    *(ref[side, here, :] for ref in held),
                    gate_up_grad[:, pl.ds(side * hidden, hidden)],
                    rates[index],
                    clip,
                )
        else:
            first_new[...], second_new[...], weight_new[...] = adam_step(
                *(ref[here, :] for ref in held), grads[index], rates[index], clip
            )


def adam_all(limit, total, gains_grad, gains, grads, weights):
    rows = grads[0].shape[0]
    tile = 32 if rows % 32 == 0 else rows

    def spec(array):
        if array.ndim == 3:
            return pl.BlockSpec((2, tile, array.shape[2]), lambda i: (0, i, 0))
        return pl.BlockSpec((tile, array.shape[1]), lambda i: (i, 0))

    def fixed(array):
        return pl.BlockSpec(array.shape, lambda i: (0, 0))

    return pl.pallas_call(
        functools.partial(adam_kernel, limit),
        grid=(rows // tile,),
        out_shape=tuple(jax.ShapeDtypeStruct(array.shape, F32) for array in (*weights, *gains))
        + (jax.ShapeDtypeStruct((1,), F32),),
        in_specs=[fixed(array) for array in (total, gains_grad, *gains)]
        + [spec(array) for array in grads]
        + [pl.BlockSpec(memory_space=pltpu.VMEM)] * len(weights),
        out_specs=tuple(spec(array) for array in weights)
        + tuple(fixed(array) for array in gains)
        + (pl.BlockSpec(memory_space=pltpu.SMEM),),
        compiler_params=pltpu.CompilerParams(vmem_limit_bytes=24 << 20),
        cost_estimate=LIGHT,
        name="adam_all",
    )(total, gains_grad, *gains, *grads, *weights)


def per_device(
    tokens,
    prefix,
    cotangent,
    query_weight,
    query_first,
    query_second,
    keyval_weight,
    keyval_first,
    keyval_second,
    outproj_weight,
    outproj_first,
    outproj_second,
    gate_up_weight,
    gate_up_first,
    gate_up_second,
    down_weight,
    down_first,
    down_second,
    norm_gains,
    gains_first,
    gains_second,
):
    replica_count = lax.axis_size("dp")
    rows_local, width = tokens.shape[1:]
    length = rows_local * TENSOR
    share, query_columns = query_weight.shape
    hidden = gate_up_weight.shape[2]
    assert tokens.shape[0] == 1 and lax.axis_size("tensor") == TENSOR
    assert rows_local == BLOCK and query_columns == Q_COLS
    TRAIL[0] = None
    place = lax.dynamic_index_in_dim(
        jnp.asarray(place_table(replica_count)), lax.axis_index(("dp", "tensor")), 0, False
    )
    cosine, sine = (jnp.asarray(table) for table in rope_tables(length))
    tokens, cotangent = tokens[0], cotangent[0]
    block_low, block_float = ((BLOCK, width), BF), ((BLOCK, width), F32)
    half_length = 2 * BLOCK

    first_columns = KV_COLS + 2 * Q_COLS + GAIN_COLS
    first = Gather(
        call(
            "cast_first",
            cast_first_body,
            [((share, first_columns), BF)],
            [keyval_weight, query_weight, outproj_weight.T, norm_gains],
            [place],
            mib=56,
        )
    )
    (token_low,) = relay(tokens)
    token_near, token_far = swap(token_low, 1), swap(token_low, 2)
    first.forward()
    first.forward()
    token_blocks = [
        token_low,
        token_near,
        token_far,
        swap(relay(token_far, deps=first.pieces[3:5])[0], 1),
    ]
    (cot_low,) = relay(cotangent)
    cot_near, cot_far = swap(cot_low, 1), swap(cot_low, 2)
    first.halve()
    cot_blocks = [cot_low, cot_near, cot_far, swap(relay(cot_far)[0], 1)]
    second = Gather(
        call(
            "cast_mlp",
            cast_mlp_body,
            [((share, 3 * hidden), BF)],
            [gate_up_weight, down_weight.T],
            deps=first.pieces[-2:],
        )
    )

    heads_low = ((Q_COLS, half_length), BF)
    logs = ((8, half_length), F32)
    (
        first_full,
        out_full,
        gains,
        rows_one,
        inv_rows,
        q,
        k,
        v,
        k_rows,
        v_rows,
        o_far,
        lse_far,
        far_keep,
        far_send,
    ) = call(
        "front",
        functools.partial(front_body, len(first.pieces)),
        [
            ((width, first_columns), BF),
            ((width, Q_COLS), BF),
            ((8, width), F32),
            ((length, width), BF),
            ((length, 1), F32),
            ((Q_COLS, length), BF),
            ((PAIR * HD, length), BF),
            ((PAIR * HD, length), BF),
            ((PAIR, length, HD), BF),
            ((PAIR, length, HD), BF),
            heads_low,
            logs,
            block_low,
            block_low,
        ],
        [*first.pieces, *token_blocks, cosine, sine],
        [place, prefix],
        mib=32,
        far=(0, 3),
    )
    far_sum = call("far_sum", add_body, [block_low], [far_keep, swap(far_send, 1)])
    attn_far = swap(far_sum, 2)
    second.relay()
    o_near, lse_near, near_keep, near_send = call(
        "near",
        near_body,
        [heads_low, logs, block_low, block_low],
        [q, k_rows, v, out_full],
        [place, prefix],
        deps=[cot_near, cot_blocks[3]],
    )
    near_got = swap(near_send, 1)
    second.relay([attn_far])
    mixed_one, rows_two = call(
        "norm",
        norm_body,
        [block_float, block_low],
        [tokens, near_keep, near_got, attn_far, gains],
        far=(0,),
    )
    two_near, two_far = swap(rows_two, 1), swap(rows_two, 2)
    a2 = [rows_two, two_near, two_far, swap(relay(two_far)[0], 1)]
    second.halve()
    mlp_full = second.place(place, width)
    mlp_out = [((half_length, hidden), BF)] * 3
    gate_near, up_near, hidden_near = call(
        "hidden_near", hidden_body, mlp_out, [rows_two, two_near, mlp_full]
    )
    gate_far, up_far, hidden_far = call(
        "hidden_far", hidden_body, mlp_out, [a2[2], a2[3], mlp_full]
    )
    down_grad = column_grad(cot_blocks, [hidden_near, hidden_far])
    down_ring = Scatter(down_grad, place)
    back_out = [((half_length, 2 * hidden), BF), block_low, block_low]
    grads_far, far_keep, far_send = call(
        "hidden_back_far",
        hidden_back_body,
        back_out,
        [cot_blocks[2], cot_blocks[3], mlp_full, gate_far, up_far],
    )
    far_got = swap(far_send, 1)
    down_ring.step()
    far_sum = call("far_sum", add_body, [block_low], [far_keep, far_got])
    part_far = swap(far_sum, 2)
    grads_near, near_keep, near_send = call(
        "hidden_back_near",
        hidden_back_body,
        back_out,
        [cot_blocks[0], cot_blocks[1], mlp_full, gate_near, up_near],
    )
    near_got = swap(near_send, 1)
    gate_up_grad = column_grad(a2, [grads_near, grads_far])
    down_ring.step()
    gate_up_ring = Scatter(gate_up_grad, place, [part_far])
    mixed_grad, mixed_low, gain_two = call(
        "norm_back",
        norm_back_body,
        [block_float, block_low, ((8, width), F32)],
        [near_keep, near_got, part_far, mixed_one, cotangent, gains],
        far=(0,),
    )
    mixed_near, mixed_far = swap(mixed_low, 1), swap(mixed_low, 2)
    sums = [((PAIR, length, HD), F32)] * 2
    held = [pltpu.VMEM((Q_COLS, half_length), BF)]
    dq_near, dk, dv = call(
        "attention_back_near",
        back_near_body,
        [heads_low, *sums],
        [mixed_low, mixed_near, out_full, q, k, k_rows, v_rows, o_near, lse_near, cosine, sine],
        [place, prefix],
        scratch=held,
    )
    gate_up_ring.step()
    down_ring.step()
    mixed = [mixed_low, mixed_near, mixed_far, swap(relay(mixed_far)[0], 1)]
    parts = call(
        "down_part",
        down_body,
        [block_low] * TENSOR,
        [hidden_near, hidden_far, mlp_full],
    )
    out_got = [swap(parts[1], 1), swap(parts[3], 1)]
    gate_up_ring.step()
    out_send = call(
        "out_send", add_body, [block_low], [parts[2], out_got[1]], deps=out_got[:1]
    )
    out_far = swap(out_send, 2)
    dq_far, dkv = call(
        "attention_back_far",
        back_far_body,
        [heads_low, ((KV_COLS, length), BF)],
        [
            *(mixed[2], mixed[3], out_full, q, k, k_rows, v_rows, o_far, lse_far, cosine, sine),
            *(dk, dv),
        ],
        [place, prefix],
        scratch=[pltpu.VMEM((PAIR, length, HD), F32)] * 2 + held,
    )
    gate_up_ring.step(down_ring.got)
    one_keep, one_far_keep, one_sends, last = last_grad(
        rows_one,
        mixed,
        token_blocks,
        inv_rows,
        first_full,
        dkv,
        (dq_near, dq_far),
        (o_near, o_far),
        gain_two,
        (),
    )
    last_ring = Scatter(last, place, [*gate_up_ring.got, out_far])
    gate_up_sum, gate_up_squares = ring_kernel(
        "gate_up_sum",
        sum_body,
        [((share, 2 * hidden), F32), ((1,), F32)],
        place,
        gate_up_ring.terms[0],
        (0,),
        gate_up_ring.terms[1:],
    )
    down_sum, down_squares = ring_kernel(
        "down_sum",
        sum_body,
        [((share, hidden), F32), ((1,), F32)],
        place,
        down_ring.terms[0],
        (0,),
        down_ring.terms[1:],
    )
    last_ring.step()
    one_got = swap(relay(one_sends)[0], 1)
    one_send = call("one_send", add_second_body, [block_low], [one_far_keep, one_got])
    one_far = swap(one_send, 2)
    last_ring.step()
    held_weights = hold(
        (
            *(query_weight, query_first, query_second),
            *(keyval_weight, keyval_first, keyval_second),
            *(outproj_weight.T, outproj_first.T, outproj_second.T),
            gate_up_weight,
        ),
    )
    last_ring.step()
    held_weights += hold(
        (gate_up_first, gate_up_second, down_weight.T, down_first.T, down_second.T)
    )
    output = call(
        "output", output_body, [block_low], [parts[0], out_got[0], out_far, mixed_one], far=(0,)
    )
    last_sum, shared = ring_kernel(
        "pack",
        pack_body,
        [((share, first_columns), F32), ((share, KV_COLS + GAIN_COLS), BF)],
        place,
        last_ring.terms[0],
        (0,),
        last_ring.terms[1:],
        [gate_up_squares, down_squares],
    )
    shared_blocks = gather_blocks(shared)
    input_grad = call(
        "input_grad",
        input_grad_body,
        [block_float],
        [one_keep, one_got, one_far, tokens, mixed_grad, gains],
        far=(0,),
    )
    keyval_total, gains_total, squares = call(
        "shared_sums",
        shared_body,
        [((share, 2 * KV * HD), F32), ((8, share), F32), ((8, 128), F32)],
        shared_blocks,
        [place],
        scratch=[pltpu.VMEM((TENSOR, share, KV_COLS + GAIN_COLS), F32)],
    )
    square_total = sum_over_dp(squares)
    params_all = D * HEADS * HD + 2 * D * KV * HD + HEADS * HD * D + 2 * D * FF + FF * D + 2 * D
    limit = 0.01 * math.sqrt(replica_count * length * params_all)
    updates = adam_all(
        limit,
        square_total,
        gains_total,
        (norm_gains, gains_first, gains_second),
        (keyval_total, last_sum, gate_up_sum, down_sum),
        held_weights,
    )
    return (
        output[None],
        input_grad[None],
        *updates[:6],
        *(update.T for update in updates[6:9]),
        *updates[9:12],
        *(update.T for update in updates[12:15]),
        *updates[15:18],
        updates[18][0],
    )


def solution(mesh):
    rows = P("dp", "tensor", None)
    weights = (
        (P("dp", "tensor"),) * 3
        + (P("dp", None),) * 3
        + (P("tensor", "dp"),) * 3
        + (P(None, "dp", "tensor"),) * 3
        + (P("tensor", "dp"),) * 3
        + (P(None, "dp"),) * 3
    )
    return jax.shard_map(
        per_device,
        mesh=mesh,
        in_specs=(rows, P("dp"), rows) + weights,
        out_specs=(rows, rows) + weights + (P(),),
        check_vma=False,
    )
```
